128 devices in a mesh: row: 8 (over x_lo, z), col: 16 (over x_hi, y, core).
Axes of the slice: x: 4 (x_hi: 2, x_lo: 2; x = x_hi * 2 + x_lo), y: 4, z: 4, core: 2. Of those that a mesh axis runs over, the one named last changes fastest.
Arguments:
- pair_tensor: float32 [768, 768, 128], P(('row', 'col')), may hold values from -30 to 30
- token_mask: int32 [768], replicated, may hold values from 0 to 1, as said below
- ln_gain: float32 [2, 128], replicated, may hold values from 0.5 to 1.5
- ln_shift: float32 [2, 128], replicated, may hold values from -3 to 3
- w_query: float32 [2, 128, 128], replicated, may hold values from -5 to 5
- w_key: float32 [2, 128, 128], replicated, may hold values from -5 to 5
- w_value: float32 [2, 128, 128], replicated, may hold values from -0.5 to 0.5
- w_bias: float32 [2, 4, 128], replicated, may hold values from -0.5 to 0.5
- w_gate: float32 [2, 128, 128], replicated, may hold values from -0.5 to 0.5
- gate_shift: float32 [2, 128], replicated, may hold values from -4 to 4
- w_out: float32 [2, 128, 128], replicated, may hold values from -0.5 to 0.5
Outputs:
- updated_pair: float32 [768, 768, 128], P(('row', 'col'))
The draws below stay inside these ranges and needn't reach their ends.
Inputs may be any that keep to these rules, and one draw needn't show every extreme that they name: Real tokens come first: token_mask is 1 on a leading run of tokens and 0 after it; token 0 is real and token 767 is padding.
All inputs are finite; a program needn't handle non-finite values.
Results may differ from the reference program's by a relative error of at most 0.00055.
Values may be sent and summed in bfloat16 or wider, within the bound.
No kernel may reach another device: no remote copies, remote signals or barrier semaphores. Data moves between devices by JAX's collectives and lax.ppermute only.
A program may use at most 128 MiB of HBM per device.

```python
import math
import jax
import jax.numpy as jnp
from jax import lax

C = 128
HEADS = 4
HEAD_DIM = 32
HD = 128
TOKENS = 768


def drawn_weight(key):
    noise_field = jax.random.truncated_normal(key, -4.0, 4.0, (2, C, HD), jnp.float32) * C ** (-0.5)
    return noise_field


def draw_w_query(key, part):
    key = jax.random.fold_in(key, 21)
    return drawn_weight(key)


def draw_w_key(key, part):
    key = jax.random.fold_in(key, 22)
    return drawn_weight(key)


def draw_token_mask(key, part):
    key = jax.random.fold_in(key, 5)
    real_count = jax.random.randint(key, (), 1, TOKENS)
    return (jnp.arange(TOKENS) < real_count).astype(jnp.int32)


def draw_pair_tensor(key, part):
    key = jax.random.fold_in(key, 11)
    key_list = jax.random.split(key, 4)
    lower = math.log(0.3)
    upper = math.log(3.0)
    cell_scale = jnp.exp(jax.random.uniform(key_list[0], (TOKENS, TOKENS, 1), jnp.float32, lower, upper))
    chan_scale = jnp.exp(jax.random.uniform(key_list[1], (C,), jnp.float32, lower, upper))
    noise_field = jax.random.truncated_normal(key_list[3], -3.0, 3.0, (TOKENS, TOKENS, C), jnp.float32)
    return noise_field * cell_scale * chan_scale


def normal_values(key, shape, width, most, kind=jnp.bfloat16):
    result = width * jax.random.normal(key, shape, jnp.float32)
    return jnp.clip(result, min=-most, max=most).astype(kind)


def setup_inputs(seed: int = 0) -> dict:
    streams_of = jax.random.split(jax.random.key(seed), 12)
    return {
        "pair_tensor": draw_pair_tensor(jax.random.fold_in(streams_of[11], 71), 0),
        "token_mask": draw_token_mask(jax.random.fold_in(streams_of[11], 71), 0),
        "ln_gain": jnp.clip(1.0 + 0.1 * jax.random.normal(streams_of[2], (2, C), jnp.float32), 0.5, 1.5),
        "ln_shift": normal_values(streams_of[3], (2, C), 0.5, 3.0, jnp.float32),
        "w_query": draw_w_query(jax.random.fold_in(streams_of[11], 71), 0),
        "w_key": draw_w_key(jax.random.fold_in(streams_of[11], 71), 0),
        "w_value": normal_values(streams_of[6], (2, C, HD), C ** -0.5, 0.5, jnp.float32),
        "w_bias": normal_values(streams_of[7], (2, HEADS, C), C ** -0.5, 0.5, jnp.float32),
        "w_gate": normal_values(streams_of[8], (2, C, HD), C ** -0.5, 0.5, jnp.float32),
        "gate_shift": normal_values(streams_of[9], (2, HD), 1.0, 4.0, jnp.float32),
        "w_out": normal_values(streams_of[10], (2, HD, C), HD ** -0.5, 0.5, jnp.float32),
    }


EPSILON = 1e-05
NEGATIVE = -1e+30
PRECISE = lax.Precision.HIGHEST

def normalize(values, gain, shift):
    centre = lax.optimization_barrier(jnp.mean(values, axis=-1, keepdims=True))
    centred = values - centre
    spread = lax.optimization_barrier(jnp.mean(centred * centred, axis=-1, keepdims=True))
    return centred * lax.rsqrt(spread + EPSILON) * gain + shift

def attend(query_rows, key_rows, value_rows, bias, live_keys):
    queries = query_rows.reshape(-1, HEADS, HEAD_DIM)
    key_split = key_rows.reshape(-1, HEADS, HEAD_DIM)
    value_split = value_rows.reshape(-1, HEADS, HEAD_DIM)
    scores = jnp.einsum('jhd,khd->hjk', queries, key_split, precision=PRECISE) + bias
    scores = jnp.where(live_keys, scores, NEGATIVE)
    highest = lax.optimization_barrier(jnp.max(scores, axis=-1, keepdims=True))
    weights = jnp.where(live_keys, jnp.exp(scores - highest), 0.0)
    shares = weights / lax.optimization_barrier(jnp.sum(weights, axis=-1, keepdims=True))
    mixed_heads = jnp.einsum('hjk,khd->jhd', shares, value_split, precision=PRECISE)
    return mixed_heads.reshape(mixed_heads.shape[0], HEADS * HEAD_DIM)

def bias_plane(pair_rows, gain, shift, weight):

    def one_row(row_cells):
        normed = normalize(row_cells, gain, shift)
        return jnp.einsum('nc,hc->hn', normed, weight, precision=PRECISE).astype(jnp.bfloat16)
    planes = lax.map(one_row, pair_rows)
    return jnp.transpose(planes, (1, 0, 2))

def pass_rows(pair_rows, plane, live_keys, gain, shift, w_q, w_k, w_v, w_g, g_shift, w_o):
    bias = plane.astype(jnp.float32)

    def one_row(row_cells):
        normed = normalize(row_cells, gain, shift)
        query = jnp.dot(normed, w_q, precision=PRECISE, preferred_element_type=jnp.float32) * HEAD_DIM ** (-0.5)
        key_rows = jnp.dot(normed, w_k, precision=PRECISE, preferred_element_type=jnp.float32)
        value_rows = jnp.dot(normed, w_v, precision=PRECISE, preferred_element_type=jnp.float32)
        gate = jax.nn.sigmoid(jnp.dot(normed, w_g, precision=PRECISE, preferred_element_type=jnp.float32) + g_shift)
        mixed = attend(query, key_rows, value_rows, bias, live_keys)
        return row_cells + jnp.dot(gate * mixed, w_o, precision=PRECISE, preferred_element_type=jnp.float32)
    return lax.map(one_row, pair_rows)

def reference(pair_tensor, token_mask, ln_gain, ln_shift, w_query, w_key, w_value, w_bias, w_gate, gate_shift, w_out):
    live_keys = token_mask > 0
    start_plane = bias_plane(pair_tensor, ln_gain[0], ln_shift[0], w_bias[0])
    first = pass_rows(pair_tensor, start_plane, live_keys, ln_gain[0], ln_shift[0], w_query[0], w_key[0], w_value[0], w_gate[0], gate_shift[0], w_out[0])
    end_plane = bias_plane(first, ln_gain[1], ln_shift[1], w_bias[1])
    flipped = jnp.swapaxes(first, 0, 1)
    second = pass_rows(flipped, jnp.swapaxes(end_plane, 1, 2), live_keys, ln_gain[1], ln_shift[1], w_query[1], w_key[1], w_value[1], w_gate[1], gate_shift[1], w_out[1])
    return jnp.swapaxes(second, 0, 1)
```

```python
import functools

import jax
import jax.numpy as jnp
import numpy as np
from jax import lax
from jax.experimental import pallas as pl
from jax.experimental.pallas import tpu as pltpu
from jax.sharding import PartitionSpec as P

HEADS = 4
HEAD_DIM = 32
HD = 128
TOKENS = 768
ROWS = 6
DEVICES = 128
EPSILON = 1e-05
NEGATIVE = -1e30
LOG2E = 1.4426950408889634
AXES = ("row", "col")
VMEM = 60 * 1024 * 1024
F32, BF16 = jnp.float32, jnp.bfloat16
NT = (((1,), (1,)), ((), ()))
NN = (((1,), (0,)), ((), ()))


def coords(device):
    row, col = divmod(device, 16)
    x_lo, z = divmod(row, 4)
    x_hi, rest = divmod(col, 8)
    y, core = divmod(rest, 2)
    return [x_hi * 2 + x_lo, y, z, core]


def device_at(x, y, z, core):
    return ((x % 2) * 4 + z) * 16 + (x // 2) * 8 + y * 2 + core


def shifted(values, axis, step):
    pairs = []
    for source in range(DEVICES):
        place = coords(source)
        place[axis] = (place[axis] + step) % (2 if axis == 3 else 4)
        pairs.append((source, device_at(*place)))
    return lax.ppermute(values, AXES, pairs)


def ring(block, axis):
    return jnp.concatenate(
        [block, shifted(block, axis, 1), shifted(block, axis, 2), shifted(block, axis, -1)], 0
    )


def gather_plane(local):
    pieces = []
    for piece in range(3):
        block = local[None, :, piece * 128 : (piece + 1) * 128]
        for stage in range(3):
            block = ring(block, (piece + stage) % 3)
        pieces += [block, shifted(block, 3, 1)]
    return pieces


def split(values):
    high = values.astype(BF16)
    return high, (values - high.astype(F32)).astype(BF16)


def dot(a, b, dims=NN):
    return lax.dot_general(a, b, dims, preferred_element_type=F32)


def dot3(a, b, dims=NN):
    (a_high, a_low), (b_high, b_low) = a, b
    return dot(a_high, b_high, dims) + (dot(a_low, b_high, dims) + dot(a_high, b_low, dims))


def normalize(values, gain, shift):
    centred = values - jnp.mean(values, axis=-1, keepdims=True)
    spread = jnp.mean(centred * centred, axis=-1, keepdims=True)
    return centred * lax.rsqrt(spread + EPSILON) * gain + shift


def put_bias(normed_pair, w_bias, rows_ref, row):
    bias = dot3(split(w_bias), normed_pair, NT)
    for half in range(2):
        at = half * 24 + row * 4
        rows_ref[at : at + 4, :] = bias[:, half * 384 : (half + 1) * 384]


def bias_kernel(x_ref, gain_ref, shift_ref, w_ref, out_ref, rows_ref):
    for row in range(ROWS):
        normed = normalize(x_ref[row], gain_ref[...], shift_ref[...])
        put_bias(split(normed), w_ref[...], rows_ref, row)
    out_ref[...] = rows_ref[...].astype(BF16)


def first_bias(x, gain, shift, w_bias):
    return pl.pallas_call(
        bias_kernel,
        out_shape=jax.ShapeDtypeStruct((48, 384), BF16),
        scratch_shapes=[pltpu.VMEM((48, 384), F32)],
        compiler_params=pltpu.CompilerParams(vmem_limit_bytes=VMEM),
        cost_estimate=pl.CostEstimate(flops=10**8, bytes_accessed=2 * 10**6, transcendentals=0),
    )(x, gain, shift, w_bias)


def lane_group():
    return lax.broadcasted_iota(jnp.int32, (1, HD), 1) // HEAD_DIM


def repeated(weight, head):
    group = lane_group()
    out = weight
    for g in range(HEADS):
        if g != head:
            out = jnp.where(group == g, pltpu.roll(weight, (HEAD_DIM * (g - head)) % HD, 1), out)
    return jnp.where(group == head, weight, out)


def arranged(w_q, w_k, w_v, w_g):
    group = lane_group()
    q = [repeated(w_q * (HEAD_DIM**-0.5 * LOG2E), h) for h in range(HEADS)]
    k = [repeated(w_k, h) for h in range(HEADS)]
    v = [
        jnp.where((group == h) | (group == h ^ 1), repeated(w_v, h), 0.0) for h in range(HEADS)
    ]
    return split(jnp.concatenate(q + k + v + [w_g], axis=1))


def project(normed, w_high, w_low, g_shift, q_ref, k_ref, v_ref):
    group = lane_group()
    n_high, n_low = normed

    def columns(at, size):
        high, low = w_high[:, at : at + size], w_low[:, at : at + size]
        return dot(n_high, high) + (dot(n_low, high) + dot(n_high, low))

    for head in range(HEADS):
        high, low = split(columns(head * HD, HD))
        q_ref[head] = jnp.where((group == 0) | (group == 2), high, low)
        high, low = split(columns((4 + head) * HD, HD))
        k_ref[head] = jnp.where(group < 2, high, low)
        high, low = split(columns((8 + head) * HD, HD))
        ones = jnp.where((group == head) | (group == head ^ 1), low, jnp.ones_like(low))
        v_ref[head] = jnp.where(group == head, high, ones)
    return jax.nn.sigmoid(columns(12 * HD, HD) + g_shift)


def build_plane(place_ref, piece_refs, live_ref, plane_ref, turned):
    mine = [place_ref[i] for i in range(4)]
    to = lax.broadcasted_iota(jnp.int32, (192, 192), 0)
    of = lax.broadcasted_iota(jnp.int32, (192, 192), 1)
    half, head, y, core, row = to // 96, (to // 24) % 4, (to // 12) % 2, (to // 6) % 2, to % 6
    slot = jnp.where(core == mine[3], 0, 1)
    source = ((y * 2 + slot) * 2 + half) * 24 + row * 4 + head
    order = jnp.where(of == source, 1.0, 0.0).astype(BF16)

    def one_group(group, _):
        y_pair, x_hi = group % 2, (group // 2) % 2
        z, x_lo = (group // 4) % 4, group // 16
        for piece in range(3):
            own, other = piece_refs[2 * piece], piece_refs[2 * piece + 1]
            chunks = []
            for y_lo in range(2):
                behind = [
                    (mine[0] - (x_hi * 2 + x_lo)) & 3,
                    (mine[1] - (y_pair * 2 + y_lo)) & 3,
                    (mine[2] - z) & 3,
                ]
                at = behind[piece] + 4 * behind[(piece + 1) % 3] + 16 * behind[(piece + 2) % 3]
                chunks += [own[at], other[at]]
            ordered = dot(order, jnp.concatenate(chunks, axis=0))
            for part in range(8):
                half_at, head_at = part // 4, part % 4
                lane = half_at * 384 + piece * 128
                plane_ref[
                    head_at, pl.ds(pl.multiple_of(group * 24, 8), 24), lane : lane + 128
                ] = ordered[part * 24 : (part + 1) * 24]
        return 0

    lax.fori_loop(0, 32, one_group, 0)
    live = live_ref[...] > 0

    def finish(head, _):
        if turned:
            for a in range(6):
                for b in range(a, 6):
                    aa, bb = slice(a * 128, a * 128 + 128), slice(b * 128, b * 128 + 128)
                    upper = plane_ref[head, aa, bb]
                    lower = plane_ref[head, bb, aa]
                    plane_ref[head, aa, bb] = jnp.where(live[:, bb], lower.T * LOG2E, NEGATIVE)
                    if a != b:
                        plane_ref[head, bb, aa] = jnp.where(live[:, aa], upper.T * LOG2E, NEGATIVE)
        else:
            plane_ref[head] = jnp.where(live, plane_ref[head] * LOG2E, NEGATIVE)
        return 0

    lax.fori_loop(0, HEADS, finish, 0)


QBLOCK = 256


def attend(keys, q_ref, k_ref, v_ref, plane_ref, mixed_ref):
    group = lane_group()

    def one_block(step, _):
        at = pl.multiple_of(step * QBLOCK, QBLOCK)
        rows = pl.ds(at, QBLOCK)
        merged = jnp.zeros((QBLOCK, HD), F32)
        for head in range(HEADS):
            scores = dot(q_ref[head, rows, :], k_ref[head, :keys, :], NT)
            scores = scores + plane_ref[head, rows, :keys]
            highest = jnp.max(scores, axis=-1, keepdims=True)
            weights = jnp.exp2(scores - highest).astype(BF16)
            mixed = dot(weights, v_ref[head, :keys, :])
            aside = HEAD_DIM * 3 if head % 2 == 0 else HEAD_DIM
            total = pltpu.roll(mixed, 2 * HEAD_DIM, 1)
            value = (mixed + pltpu.roll(mixed, aside, 1)) / total
            merged = jnp.where(group == head, value, merged)
        mixed_ref[rows, :] = merged
        return 0

    lax.fori_loop(0, TOKENS // QBLOCK, one_block, 0)


def pass_kernel(
    turned, with_bias, scalar_ref, x_ref, live_ref, vec_ref, wq_ref, wk_ref, wv_ref, wg_ref, wo_ref,
    nvec_ref, nbias_ref, *rest,
):
    piece_refs, rest = rest[:6], rest[6:]
    outs, rest = rest[: 2 if with_bias else 1], rest[2 if with_bias else 1 :]
    plane_ref, wh_ref, wl_ref, q_ref, k_ref, v_ref, mixed_ref = rest[:7]
    step = pl.program_id(0)

    @pl.when(step == 0)
    def _():
        w_high, w_low = arranged(wq_ref[...], wk_ref[...], wv_ref[...], wg_ref[...])
        wh_ref[...] = w_high
        wl_ref[...] = w_low
        build_plane(scalar_ref, piece_refs, live_ref, plane_ref, turned)

    x = x_ref[0]
    normed = normalize(x, vec_ref[0:1, :], vec_ref[1:2, :])
    gate = project(split(normed), wh_ref, wl_ref, vec_ref[2:3, :], q_ref, k_ref, v_ref)
    real = scalar_ref[4]
    for keys in (256, 512, 768):

        @pl.when((real > keys - 256) & (real <= keys))
        def _():
            attend(keys, q_ref, k_ref, v_ref, plane_ref, mixed_ref)

    update = dot3(split(gate * mixed_ref[...]), split(wo_ref[...]))
    if with_bias:
        first = x + update
        outs[0][0] = first
        rows_ref = rest[7]
        normed = normalize(first, nvec_ref[0:1, :], nvec_ref[1:2, :])
        bias = dot3(split(nbias_ref[...]), split(normed), NT)
        for half in range(2):
            for row in range(ROWS):

                @pl.when(step == row)
                def _():
                    at = half * 24 + row * 4
                    rows_ref[at : at + 4, :] = bias[:, half * 384 : (half + 1) * 384]

        @pl.when(step == ROWS - 1)
        def _():
            outs[1][...] = rows_ref[...].astype(BF16)
    else:
        outs[0][0] = update


def run_pass(turned, scalars, x, live, vecs, w_q, w_k, w_v, w_g, w_o, pieces, nvecs=None, nbias=None):
    with_bias = nvecs is not None
    if not with_bias:
        nvecs, nbias = vecs, jnp.zeros((HEADS, HD), F32)
    whole = pl.BlockSpec(memory_space=pltpu.VMEM)
    row_spec = pl.BlockSpec((1, TOKENS, HD), lambda i: (i, 0, 0))
    out_shape = [jax.ShapeDtypeStruct((ROWS, TOKENS, HD), F32)]
    out_specs = [row_spec]
    scratch = [
        pltpu.VMEM((HEADS, TOKENS, TOKENS), F32),
        pltpu.VMEM((HD, 13 * HD), BF16),
        pltpu.VMEM((HD, 13 * HD), BF16),
        pltpu.VMEM((HEADS, TOKENS, HD), BF16),
        pltpu.VMEM((HEADS, TOKENS, HD), BF16),
        pltpu.VMEM((HEADS, TOKENS, HD), BF16),
        pltpu.VMEM((TOKENS, HD), F32),
    ]
    if with_bias:
        out_shape.append(jax.ShapeDtypeStruct((48, 384), BF16))
        out_specs.append(pl.BlockSpec((48, 384), lambda i: (0, 0)))
        scratch.append(pltpu.VMEM((48, 384), F32))
    return pl.pallas_call(
        functools.partial(pass_kernel, turned, with_bias),
        grid=(ROWS,),
        in_specs=[pl.BlockSpec(memory_space=pltpu.SMEM), row_spec] + [whole] * 15,
        out_specs=out_specs,
        out_shape=out_shape,
        scratch_shapes=scratch,
        compiler_params=pltpu.CompilerParams(
            vmem_limit_bytes=VMEM, dimension_semantics=("arbitrary",)
        ),
        cost_estimate=pl.CostEstimate(
            flops=2 * 10**10, bytes_accessed=10**7, transcendentals=14 * 10**6
        ),
    )(scalars, x, live, vecs, w_q, w_k, w_v, w_g, w_o, nvecs, nbias, *pieces)


def on_device(
    pair_tensor,
    token_mask,
    ln_gain,
    ln_shift,
    w_query,
    w_key,
    w_value,
    w_bias,
    w_gate,
    gate_shift,
    w_out,
):
    row, col = lax.axis_index("row"), lax.axis_index("col")
    place = [(col // 8) * 2 + row // 4, (col // 2) % 4, row % 4, col % 2]
    scalars = jnp.stack([jnp.int32(p) for p in place] + [jnp.sum(token_mask, dtype=jnp.int32)])
    live = token_mask.reshape(1, TOKENS)
    vecs = [jnp.stack([ln_gain[p], ln_shift[p], gate_shift[p]]) for p in range(2)]

    def weights(p):
        return w_query[p], w_key[p], w_value[p], w_gate[p], w_out[p]

    start_rows = first_bias(pair_tensor, ln_gain[0:1], ln_shift[0:1], w_bias[0])
    first, end_rows = run_pass(
        False, scalars, pair_tensor, live, vecs[0], *weights(0), gather_plane(start_rows),
        vecs[1], w_bias[1],
    )
    columns = lax.all_to_all(
        jnp.swapaxes(first, 0, 1), AXES, split_axis=0, concat_axis=1, tiled=True
    )
    (update,) = run_pass(
        True, scalars, columns, live, vecs[1], *weights(1), gather_plane(end_rows)
    )
    returned = lax.all_to_all(
        update.astype(jnp.float16), AXES, split_axis=1, concat_axis=0, tiled=True
    )
    return first + jnp.swapaxes(returned, 0, 1).astype(F32)


def solution(mesh):
    placed = (P(AXES, None, None), P(), P(), P(), P(), P(), P(), P(), P(), P(), P())
    return jax.shard_map(
        on_device,
        mesh=mesh,
        in_specs=placed,
        out_specs=P(AXES, None, None),
        check_vma=False,
    )
```

```python
import functools

import jax
import jax.numpy as jnp
import numpy as np
from jax import lax
from jax.experimental import pallas as pl
from jax.experimental.pallas import tpu as pltpu
from jax.sharding import PartitionSpec as P

HEADS = 4
HEAD_DIM = 32
HD = 128
TOKENS = 768
ROWS = 6
DEVICES = 128
PADDED = 40
EPSILON = 1e-05
NEGATIVE = -1e30
LOG2E = 1.4426950408889634
AXES = ("row", "col")
VMEM = 60 * 1024 * 1024
F32, BF16 = jnp.float32, jnp.bfloat16
NT = (((1,), (1,)), ((), ()))
NN = (((1,), (0,)), ((), ()))


def coords(device):
    row, col = divmod(device, 16)
    x_lo, z = divmod(row, 4)
    x_hi, rest = divmod(col, 8)
    y, core = divmod(rest, 2)
    return [x_hi * 2 + x_lo, y, z, core]


def device_at(x, y, z, core):
    return ((x % 2) * 4 + z) * 16 + (x // 2) * 8 + y * 2 + core


def shifted(values, axis, step):
    pairs = []
    for source in range(DEVICES):
        place = coords(source)
        place[axis] = (place[axis] + step) % (2 if axis == 3 else 4)
        pairs.append((source, device_at(*place)))
    return lax.ppermute(values, AXES, pairs)


def ring(block, axis):
    return jnp.concatenate(
        [block, shifted(block, axis, 1), shifted(block, axis, 2), shifted(block, axis, -1)], 0
    )


def merge_kernel(scalar_ref, *refs):
    to = lax.broadcasted_iota(jnp.int32, (192, 192), 0)
    of = lax.broadcasted_iota(jnp.int32, (192, 192), 1)
    head, y, core, row = to // 48, (to // 12) % 4, (to // 6) % 2, to % 6
    behind = (scalar_ref[1] - y) & 3
    source = (behind * 2 + (core ^ scalar_ref[3])) * 24 + row * 4 + head
    order = jnp.where(of == source, 1.0, 0.0).astype(BF16)
    slots = jnp.concatenate([ref[...] for ref in refs[:4]], axis=0)
    ordered = dot(order, slots).astype(BF16)
    for head_at in range(HEADS):
        refs[4 + head_at // 2][head_at % 2] = ordered[head_at * 48 : (head_at + 1) * 48]


def merge(scalars, slots):
    vmem = pl.BlockSpec(memory_space=pltpu.VMEM)
    return pl.pallas_call(
        merge_kernel,
        in_specs=[pl.BlockSpec(memory_space=pltpu.SMEM)] + [vmem] * 4,
        out_shape=[jax.ShapeDtypeStruct((2, 48, 384), BF16)] * 2,
        compiler_params=pltpu.CompilerParams(vmem_limit_bytes=VMEM),
        cost_estimate=pl.CostEstimate(flops=10**7, bytes_accessed=3 * 10**5, transcendentals=0),
    )(scalars, *slots)


def gather_plane(scalars, kept, sent):
    block = jnp.concatenate([kept, shifted(sent, 3, 1)], axis=0)
    slots = [block] + [shifted(block, 1, step) for step in (1, 2, -1)]
    pieces = []
    for pair, axes in zip(merge(scalars, slots), ((0, 2), (2, 0))):
        block = pair[None]
        for axis in axes:
            block = ring(block, axis)
        pieces += [block, shifted(block, 3, 1)]
    return pieces


def split(values):
    high = values.astype(BF16)
    return high, (values - high.astype(F32)).astype(BF16)


def dot(a, b, dims=NN):
    return lax.dot_general(a, b, dims, preferred_element_type=F32)


def dot3(a, b, dims=NN):
    (a_high, a_low), (b_high, b_low) = a, b
    return dot(a_high, b_high, dims) + (dot(a_low, b_high, dims) + dot(a_high, b_low, dims))


def dot_split(a, b_twice, b_low):
    return dot(a, b_twice) + dot(a[:, :HD], b_low)


def side_by_side(values):
    return jnp.concatenate(split(values), axis=1)


def twice(weight):
    high, low = split(weight)
    return jnp.concatenate([high, high], axis=0), low


def normalize(values, gain, shift):
    mean = jnp.full((2 * HD, HD), 1.0 / HD, BF16)
    centred = values - dot(side_by_side(values), mean)
    spread = dot(side_by_side(centred * centred), mean)
    return centred * lax.rsqrt(spread + EPSILON) * gain + shift


def put_bias(normed, w_bias, rows_ref, row):
    bias = dot3(split(w_bias), split(normed), NT)
    for half in range(2):
        at = half * 24 + row * 4
        rows_ref[at : at + 4, :] = bias[:, half * 384 : (half + 1) * 384]


def hand_over(scalar_ref, rows_ref, kept_ref, sent_ref):
    first, second = rows_ref[:24, :].astype(BF16), rows_ref[24:, :].astype(BF16)
    kept_ref[...] = jnp.where(scalar_ref[3] == 0, first, second)
    sent_ref[...] = jnp.where(scalar_ref[3] == 0, second, first)


def bias_kernel(scalar_ref, x_ref, gain_ref, shift_ref, w_ref, kept_ref, sent_ref, rows_ref):
    for row in range(ROWS):
        normed = normalize(x_ref[row], gain_ref[...], shift_ref[...])
        put_bias(normed, w_ref[...], rows_ref, row)
    hand_over(scalar_ref, rows_ref, kept_ref, sent_ref)


def first_bias(scalars, x, gain, shift, w_bias):
    vmem = pl.BlockSpec(memory_space=pltpu.VMEM)
    return pl.pallas_call(
        bias_kernel,
        in_specs=[pl.BlockSpec(memory_space=pltpu.SMEM)] + [vmem] * 4,
        out_shape=[jax.ShapeDtypeStruct((24, 384), BF16)] * 2,
        scratch_shapes=[pltpu.VMEM((48, 384), F32)],
        compiler_params=pltpu.CompilerParams(vmem_limit_bytes=VMEM),
        cost_estimate=pl.CostEstimate(flops=10**8, bytes_accessed=2 * 10**6, transcendentals=0),
    )(scalars, x, gain, shift, w_bias)


def lane_group():
    return lax.broadcasted_iota(jnp.int32, (1, HD), 1) // HEAD_DIM


def spreader(source_of):
    row = lax.broadcasted_iota(jnp.int32, (2 * HD, HEADS * HD), 0)
    column = lax.broadcasted_iota(jnp.int32, (2 * HD, HEADS * HD), 1)
    head, group, d = column // HD, (column // HEAD_DIM) % 4, column % HEAD_DIM
    part = source_of(head, group)
    hit = (part >= 0) & (row == part * HD + head * HEAD_DIM + d)
    return jnp.where(hit, 1.0, 0.0).astype(BF16)


def prepare_weights(weights, w_twice_ref, w_low_ref, spread_ref):
    for at, weight in enumerate(weights):
        high, low = twice(weight)
        w_twice_ref[:, at * HD : (at + 1) * HD] = high
        w_low_ref[:, at * HD : (at + 1) * HD] = low
    spread_ref[0] = spreader(lambda head, group: group % 2)
    spread_ref[1] = spreader(lambda head, group: group // 2)


def project_kernel(
    crossed, x_ref, vec_ref, wq_ref, wk_ref, wv_ref, wg_ref, q_ref, k_ref, v_ref, g_ref,
    w_twice_ref, w_low_ref, spread_ref, *rest,
):
    step = pl.program_id(0)

    @pl.when(step == 0)
    def _():
        weights = [wq_ref[...] * (HEAD_DIM**-0.5 * LOG2E), wk_ref[...], wv_ref[...], wg_ref[...]]
        prepare_weights(weights, w_twice_ref, w_low_ref, spread_ref)

    if crossed:
        for row in range(ROWS):
            rest[0][pl.ds(row, DEVICES, stride=ROWS), :] = x_ref[
                pl.ds(row * ROWS + step, DEVICES, stride=PADDED), :
            ]
        x = rest[0][...]
    else:
        x = x_ref[0]
    cells = side_by_side(normalize(x, vec_ref[0:1, :], vec_ref[1:2, :]))

    def columns(at):
        cut = slice(at * HD, (at + 1) * HD)
        return dot_split(cells, w_twice_ref[:, cut], w_low_ref[:, cut])

    for at, ref in enumerate((q_ref, k_ref)):
        parts = side_by_side(columns(at))
        for pair in range(2):
            cut = slice(pair * 2 * HD, (pair + 1) * 2 * HD)
            spread = dot(parts, spread_ref[at, :, cut]).astype(BF16)
            ref[0, 2 * pair] = spread[:, :HD]
            ref[0, 2 * pair + 1] = spread[:, HD:]
    v_ref[0] = side_by_side(columns(2))
    g_ref[0] = jax.nn.sigmoid(columns(3) + vec_ref[2:3, :])


def project(crossed, x, vecs, w_q, w_k, w_v, w_g):
    whole = pl.BlockSpec(memory_space=pltpu.VMEM)
    row_spec = pl.BlockSpec((1, TOKENS, HD), lambda i: (i, 0, 0))
    head_spec = pl.BlockSpec((1, HEADS, TOKENS, HD), lambda i: (i, 0, 0, 0))
    scratch = [
        pltpu.VMEM((2 * HD, 4 * HD), BF16),
        pltpu.VMEM((HD, 4 * HD), BF16),
        pltpu.VMEM((2, 2 * HD, HEADS * HD), BF16),
    ]
    if crossed:
        scratch.append(pltpu.VMEM((TOKENS, HD), F32))
    return pl.pallas_call(
        functools.partial(project_kernel, crossed),
        grid=(ROWS,),
        in_specs=[whole if crossed else row_spec] + [whole] * 5,
        out_specs=[
            head_spec, head_spec, pl.BlockSpec((1, TOKENS, 2 * HD), lambda i: (i, 0, 0)), row_spec,
        ],
        out_shape=[
            jax.ShapeDtypeStruct((ROWS, HEADS, TOKENS, HD), BF16),
            jax.ShapeDtypeStruct((ROWS, HEADS, TOKENS, HD), BF16),
            jax.ShapeDtypeStruct((ROWS, TOKENS, 2 * HD), BF16),
            jax.ShapeDtypeStruct((ROWS, TOKENS, HD), F32),
        ],
        scratch_shapes=scratch,
        compiler_params=pltpu.CompilerParams(
            vmem_limit_bytes=VMEM, dimension_semantics=("arbitrary",)
        ),
        cost_estimate=pl.CostEstimate(
            flops=10**10, bytes_accessed=17 * 10**6, transcendentals=10**6
        ),
    )(x, vecs, w_q, w_k, w_v, w_g)


def build_plane(scalar_ref, piece_refs, plane_ref, turned):
    my_x, my_z, core, real = scalar_ref[0], scalar_ref[2], scalar_ref[3], scalar_ref[4]
    limit = ((real + 255) // 256) * 256

    def one_group(group, _):
        x_hi, z, x_lo = group % 2, (group // 2) % 4, group // 8
        behind_x, behind_z = (my_x - (x_hi * 2 + x_lo)) & 3, (my_z - z) & 3
        rows = pl.ds(pl.multiple_of(group * 48, 16), 48)

        def one_half(own):
            half = core if own else 1 - core
            lanes = pl.ds(pl.multiple_of(half * 384, 128), 384)
            if turned:
                key = lax.broadcasted_iota(jnp.int32, (48, 384), 0) + group * 48
                needed = group * 48 < limit
            else:
                key = lax.broadcasted_iota(jnp.int32, (48, 384), 1) + half * 384
                needed = half * 384 < limit

            @pl.when(needed)
            def _():
                for head in range(HEADS):
                    if head < 2:
                        at = behind_z * 4 + behind_x
                    else:
                        at = behind_x * 4 + behind_z
                    values = piece_refs[head // 2 * 2 + (0 if own else 1)][at, head % 2]
                    plane_ref[head, rows, lanes] = jnp.where(
                        key < real, values.astype(F32) * LOG2E, NEGATIVE
                    )

        one_half(True)
        one_half(False)
        return 0

    lax.fori_loop(0, 16, one_group, 0)

    def turn(head, _):
        for a in range(6):

            @pl.when(a * 128 < limit)
            def _():
                for b in range(a, 6):
                    aa, bb = slice(a * 128, a * 128 + 128), slice(b * 128, b * 128 + 128)
                    upper = plane_ref[head, aa, bb]
                    lower = plane_ref[head, bb, aa]
                    plane_ref[head, aa, bb] = lower.T
                    if a != b:
                        plane_ref[head, bb, aa] = upper.T
        return 0

    if turned:
        lax.fori_loop(0, HEADS, turn, 0)


def attend(keys, q_ref, k_ref, v_ref, plane_ref, mixed_ref):
    group = lane_group()
    value = total = None
    for head in range(HEADS):
        scores = dot(q_ref[0, head], k_ref[0, head, :keys, :], NT) + plane_ref[head, :, :keys]
        highest = jnp.max(scores, axis=-1, keepdims=True)
        weights = jnp.exp2(scores - highest).astype(BF16)
        weight = jnp.sum(weights.astype(F32), axis=-1, keepdims=True)
        mixed = dot(weights, v_ref[0, :keys, :])
        mixed = mixed[:, :HD] + mixed[:, HD:]
        weight = jnp.broadcast_to(weight, mixed.shape)
        value = mixed if head == 0 else jnp.where(group == head, mixed, value)
        total = weight if head == 0 else jnp.where(group == head, weight, total)
    mixed_ref[...] = value / total


def attend_kernel(turned, scalar_ref, q_ref, k_ref, v_ref, g_ref, wo_ref, *rest):
    piece_refs, rest = rest[:4], rest[4:]
    step = pl.program_id(0)
    if turned:
        crossed_ref, plane_ref, mixed_ref = rest
    else:
        x_ref, nvec_ref, nbias_ref = rest[:3]
        first_ref, crossed_ref, kept_ref, sent_ref, plane_ref, mixed_ref, rows_ref = rest[3:]

    @pl.when(step == 0)
    def _():
        build_plane(scalar_ref, piece_refs, plane_ref, turned)

    real = scalar_ref[4]
    for keys in (256, 512, 768):

        @pl.when((real > keys - 256) & (real <= keys))
        def _():
            attend(keys, q_ref, k_ref, v_ref, plane_ref, mixed_ref)

    update = dot_split(side_by_side(g_ref[0] * mixed_ref[...]), *twice(wo_ref[...]))
    if turned:
        mixed_ref[...] = update
        for row in range(ROWS):
            crossed_ref[pl.ds(row * ROWS + step, DEVICES, stride=PADDED), :] = mixed_ref[
                pl.ds(row, DEVICES, stride=ROWS), :
            ]
    else:
        first = x_ref[0] + update
        first_ref[0] = first
        mixed_ref[...] = first
        for column in range(ROWS):
            crossed_ref[pl.ds(step * ROWS + column, DEVICES, stride=PADDED), :] = mixed_ref[
                pl.ds(column, DEVICES, stride=ROWS), :
            ]
        normed = normalize(first, nvec_ref[0:1, :], nvec_ref[1:2, :])
        bias = dot3(split(nbias_ref[...]), split(normed), NT)
        for row in range(ROWS):

            @pl.when(step == row)
            def _():
                for half in range(2):
                    at = half * 24 + row * 4
                    rows_ref[at : at + 4, :] = bias[:, half * 384 : (half + 1) * 384]

        @pl.when(step == ROWS - 1)
        def _():
            hand_over(scalar_ref, rows_ref, kept_ref, sent_ref)


def run_pass(turned, scalars, projected, w_o, pieces, x=None, nvecs=None, nbias=None):
    whole = pl.BlockSpec(memory_space=pltpu.VMEM)
    row_spec = pl.BlockSpec((1, TOKENS, HD), lambda i: (i, 0, 0))
    head_spec = pl.BlockSpec((1, HEADS, TOKENS, HD), lambda i: (i, 0, 0, 0))
    in_specs = [pl.BlockSpec(memory_space=pltpu.SMEM), head_spec, head_spec]
    in_specs += [pl.BlockSpec((1, TOKENS, 2 * HD), lambda i: (i, 0, 0)), row_spec] + [whole] * 5
    out_shape = [jax.ShapeDtypeStruct((DEVICES * PADDED, HD), F32)]
    out_specs = [pl.BlockSpec((DEVICES * PADDED, HD), lambda i: (0, 0))]
    scratch = [pltpu.VMEM((HEADS, TOKENS, TOKENS), F32), pltpu.VMEM((TOKENS, HD), F32)]
    args = [scalars, *projected, w_o, *pieces]
    if not turned:
        in_specs += [row_spec, whole, whole]
        args += [x, nvecs, nbias]
        out_shape = [jax.ShapeDtypeStruct((ROWS, TOKENS, HD), F32)] + out_shape
        out_shape += [jax.ShapeDtypeStruct((24, 384), BF16)] * 2
        out_specs = [row_spec] + out_specs + [pl.BlockSpec((24, 384), lambda i: (0, 0))] * 2
        scratch.append(pltpu.VMEM((48, 384), F32))
    return pl.pallas_call(
        functools.partial(attend_kernel, turned),
        grid=(ROWS,),
        in_specs=in_specs,
        out_specs=out_specs,
        out_shape=out_shape,
        scratch_shapes=scratch,
        compiler_params=pltpu.CompilerParams(
            vmem_limit_bytes=VMEM, dimension_semantics=("arbitrary",)
        ),
        cost_estimate=pl.CostEstimate(
            flops=2 * 10**10, bytes_accessed=2 * 10**7, transcendentals=14 * 10**6
        ),
    )(*args)


def final_kernel(first_ref, update_ref, out_ref, row_ref):
    step = pl.program_id(0)
    for column in range(ROWS):
        row_ref[pl.ds(column, DEVICES, stride=ROWS), :] = update_ref[
            pl.ds(step * ROWS + column, DEVICES, stride=PADDED), :
        ]
    out_ref[0] = first_ref[0] + row_ref[...]


def add_crossed(first, update):
    row_spec = pl.BlockSpec((1, TOKENS, HD), lambda i: (i, 0, 0))
    return pl.pallas_call(
        final_kernel,
        grid=(ROWS,),
        in_specs=[row_spec, pl.BlockSpec(memory_space=pltpu.VMEM)],
        out_specs=row_spec,
        out_shape=jax.ShapeDtypeStruct((ROWS, TOKENS, HD), F32),
        scratch_shapes=[pltpu.VMEM((TOKENS, HD), F32)],
        compiler_params=pltpu.CompilerParams(
            vmem_limit_bytes=VMEM, dimension_semantics=("arbitrary",)
        ),
        cost_estimate=pl.CostEstimate(flops=10**6, bytes_accessed=8 * 10**6, transcendentals=0),
    )(first, update)


def cross(values):
    return lax.all_to_all(values, AXES, split_axis=0, concat_axis=0, tiled=True)


def on_device(
    pair_tensor,
    token_mask,
    ln_gain,
    ln_shift,
    w_query,
    w_key,
    w_value,
    w_bias,
    w_gate,
    gate_shift,
    w_out,
):
    row, col = lax.axis_index("row"), lax.axis_index("col")
    place = [(col // 8) * 2 + row // 4, (col // 2) % 4, row % 4, col % 2]
    scalars = jnp.stack([jnp.int32(p) for p in place] + [jnp.sum(token_mask, dtype=jnp.int32)])
    vecs = [jnp.stack([ln_gain[p], ln_shift[p], gate_shift[p]]) for p in range(2)]

    def weights(p):
        return w_query[p], w_key[p], w_value[p], w_gate[p]

    start = first_bias(scalars, pair_tensor, ln_gain[0:1], ln_shift[0:1], w_bias[0])
    planes = gather_plane(scalars, *start)
    projected = project(False, pair_tensor, vecs[0], *weights(0))
    first, crossed, *end = run_pass(
        False, scalars, projected, w_out[0], planes, pair_tensor, vecs[1], w_bias[1]
    )
    columns = cross(crossed)
    planes = gather_plane(scalars, *end)
    projected = project(True, columns, vecs[1], *weights(1))
    (update,) = run_pass(True, scalars, projected, w_out[1], planes)
    return add_crossed(first, cross(update.astype(jnp.float16)).astype(F32))


def solution(mesh):
    placed = (P(AXES, None, None), P(), P(), P(), P(), P(), P(), P(), P(), P(), P())
    return jax.shard_map(
        on_device,
        mesh=mesh,
        in_specs=placed,
        out_specs=P(AXES, None, None),
        check_vma=False,
    )
```

```python
import functools

import jax
import jax.numpy as jnp
import numpy as np
from jax import lax
from jax.experimental import pallas as pl
from jax.experimental.pallas import tpu as pltpu
from jax.sharding import PartitionSpec as P

HEADS = 4
HEAD_DIM = 32
HD = 128
TOKENS = 768
ROWS = 6
DEVICES = 128
PADDED = 40
EPSILON = 1e-05
NEGATIVE = -1e30
LOG2E = 1.4426950408889634
CURVE = 4.0
CODE_STEP = float(np.log(1 + CURVE * 11.32) / 32767)
AXES = ("row", "col")
VMEM = 60 * 1024 * 1024
F32, BF16 = jnp.float32, jnp.bfloat16
NT = (((1,), (1,)), ((), ()))
NN = (((1,), (0,)), ((), ()))


def coords(device):
    row, col = divmod(device, 16)
    x_lo, z = divmod(row, 4)
    x_hi, rest = divmod(col, 8)
    y, core = divmod(rest, 2)
    return [x_hi * 2 + x_lo, y, z, core]


def device_at(x, y, z, core):
    return ((x % 2) * 4 + z) * 16 + (x // 2) * 8 + y * 2 + core


def shifted(values, axis, step):
    pairs = []
    for source in range(DEVICES):
        place = coords(source)
        place[axis] = (place[axis] + step) % (2 if axis == 3 else 4)
        pairs.append((source, device_at(*place)))
    return lax.ppermute(values, AXES, pairs)


def ring(block, axis):
    return jnp.concatenate(
        [block, shifted(block, axis, 1), shifted(block, axis, 2), shifted(block, axis, -1)], 0
    )


def merge_kernel(scalar_ref, *refs):
    to = lax.broadcasted_iota(jnp.int32, (192, 192), 0)
    of = lax.broadcasted_iota(jnp.int32, (192, 192), 1)
    head, y, core, row = to // 48, (to // 12) % 4, (to // 6) % 2, to % 6
    behind = (scalar_ref[1] - y) & 3
    source = (behind * 2 + (core ^ scalar_ref[3])) * 24 + row * 4 + head
    order = jnp.where(of == source, 1.0, 0.0).astype(BF16)
    slots = jnp.concatenate([ref[...] for ref in refs[:4]], axis=0)
    ordered = dot(order, slots).astype(BF16)
    for head_at in range(HEADS):
        refs[4 + head_at // 2][head_at % 2] = ordered[head_at * 48 : (head_at + 1) * 48]


def merge(scalars, slots):
    vmem = pl.BlockSpec(memory_space=pltpu.VMEM)
    return pl.pallas_call(
        merge_kernel,
        in_specs=[pl.BlockSpec(memory_space=pltpu.SMEM)] + [vmem] * 4,
        out_shape=[jax.ShapeDtypeStruct((2, 48, 384), BF16)] * 2,
        compiler_params=pltpu.CompilerParams(vmem_limit_bytes=VMEM),
        cost_estimate=pl.CostEstimate(flops=10**7, bytes_accessed=3 * 10**5, transcendentals=0),
    )(scalars, *slots)


def gather_plane(place, kept, sent, beside, work):
    block = jnp.concatenate([kept, shifted(sent, 3, 1)], axis=0)
    slots = [block] + [shifted(block, 1, step) for step in (1, 2, -1)]
    blocks = [ring(pair[None], axis) for pair, axis in zip(merge(place, slots), (0, 2))]
    *blocks, beside = lax.optimization_barrier((*blocks, beside))
    blocks = [ring(block, axis) for block, axis in zip(blocks, (2, 0))]
    *blocks, done = lax.optimization_barrier((*blocks, work(beside)))
    pieces = []
    for block in blocks:
        pieces += [block, shifted(block, 3, 1)]
    return pieces, done


def split(values):
    high = values.astype(BF16)
    return high, (values - high.astype(F32)).astype(BF16)


def dot(a, b, dims=NN):
    return lax.dot_general(a, b, dims, preferred_element_type=F32)


def dot3(a, b, dims=NN):
    (a_high, a_low), (b_high, b_low) = a, b
    return dot(a_high, b_high, dims) + (dot(a_low, b_high, dims) + dot(a_high, b_low, dims))


def dot_split(a, b_twice, b_low):
    return dot(a, b_twice) + dot(a[:, :HD], b_low)


def side_by_side(values):
    return jnp.concatenate(split(values), axis=1)


def twice(weight):
    high, low = split(weight)
    return jnp.concatenate([high, high], axis=0), low


def standardize(values):
    mean = jnp.full((2 * HD, HD), 1.0 / HD, BF16)
    centred = values - dot(side_by_side(values), mean)
    spread = dot(side_by_side(centred * centred), mean)
    return centred * lax.rsqrt(spread + EPSILON)


def normalize(values, gain, shift):
    return standardize(values) * gain + shift


def encode(values):
    size = jnp.floor(jnp.log(1.0 + CURVE * jnp.abs(values)) * (1 / CODE_STEP) + 0.5)
    return jnp.where(values < 0, -size, size)


def decode(codes):
    size = (jnp.exp(jnp.abs(codes) * CODE_STEP) - 1.0) * (1 / CURVE)
    return jnp.where(codes < 0, -size, size)


def put_bias(normed, w_bias, rows_ref, row):
    bias = dot3(split(w_bias), split(normed), NT)
    for half in range(2):
        at = half * 24 + row * 4
        rows_ref[at : at + 4, :] = bias[:, half * 384 : (half + 1) * 384]


def hand_over(scalar_ref, rows_ref, kept_ref, sent_ref):
    first, second = rows_ref[:24, :].astype(BF16), rows_ref[24:, :].astype(BF16)
    kept_ref[...] = jnp.where(scalar_ref[3] == 0, first, second)
    sent_ref[...] = jnp.where(scalar_ref[3] == 0, second, first)


def bias_kernel(scalar_ref, x_ref, gain_ref, shift_ref, w_ref, kept_ref, sent_ref, rows_ref):
    for row in range(ROWS):
        normed = normalize(x_ref[row], gain_ref[0:1, :], shift_ref[0:1, :])
        put_bias(normed, w_ref[0], rows_ref, row)
    hand_over(scalar_ref, rows_ref, kept_ref, sent_ref)


def first_bias(scalars, x, gain, shift, w_bias):
    vmem = pl.BlockSpec(memory_space=pltpu.VMEM)
    return pl.pallas_call(
        bias_kernel,
        in_specs=[pl.BlockSpec(memory_space=pltpu.SMEM)] + [vmem] * 4,
        out_shape=[jax.ShapeDtypeStruct((24, 384), BF16)] * 2,
        scratch_shapes=[pltpu.VMEM((48, 384), F32)],
        compiler_params=pltpu.CompilerParams(vmem_limit_bytes=VMEM),
        cost_estimate=pl.CostEstimate(flops=10**8, bytes_accessed=2 * 10**6, transcendentals=0),
    )(scalars, x, gain, shift, w_bias)


def lane_group():
    return lax.broadcasted_iota(jnp.int32, (1, HD), 1) // HEAD_DIM


def spreader(source_of):
    row = lax.broadcasted_iota(jnp.int32, (2 * HD, HEADS * HD), 0)
    column = lax.broadcasted_iota(jnp.int32, (2 * HD, HEADS * HD), 1)
    head, group, d = column // HD, (column // HEAD_DIM) % 4, column % HEAD_DIM
    part = source_of(head, group)
    hit = (part >= 0) & (row == part * HD + head * HEAD_DIM + d)
    return jnp.where(hit, 1.0, 0.0).astype(BF16)


def prepare_weights(weights, w_twice_ref, w_low_ref, spread_ref):
    for at, weight in enumerate(weights):
        high, low = twice(weight)
        w_twice_ref[:, at * HD : (at + 1) * HD] = high
        w_low_ref[:, at * HD : (at + 1) * HD] = low
    spread_ref[0] = spreader(lambda head, group: group % 2)
    spread_ref[1] = spreader(lambda head, group: group // 2)


def project_kernel(
    crossed, x_ref, gain_ref, shift_ref, gs_ref, wq_ref, wk_ref, wv_ref, wg_ref, q_ref, k_ref, v_ref, g_ref,
    w_twice_ref, w_low_ref, spread_ref, *rest,
):
    step = pl.program_id(0)

    @pl.when(step == 0)
    def _():
        weights = [wq_ref[0] * (HEAD_DIM**-0.5 * LOG2E), wk_ref[0], wv_ref[0], wg_ref[0]]
        prepare_weights(weights, w_twice_ref, w_low_ref, spread_ref)

    if crossed:
        for row in range(ROWS):
            rest[0][pl.ds(row, DEVICES, stride=ROWS), :] = x_ref[
                pl.ds(row * ROWS + step, DEVICES, stride=PADDED), :
            ]
        standard = decode(rest[0][...])
    else:
        standard = standardize(x_ref[0])
    own = slice(int(crossed), int(crossed) + 1)
    cells = side_by_side(standard * gain_ref[own, :] + shift_ref[own, :])

    def columns(at):
        cut = slice(at * HD, (at + 1) * HD)
        return dot_split(cells, w_twice_ref[:, cut], w_low_ref[:, cut])

    for at, ref in enumerate((q_ref, k_ref)):
        parts = side_by_side(columns(at))
        for pair in range(2):
            cut = slice(pair * 2 * HD, (pair + 1) * 2 * HD)
            spread = dot(parts, spread_ref[at, :, cut]).astype(BF16)
            ref[0, 2 * pair] = spread[:, :HD]
            ref[0, 2 * pair + 1] = spread[:, HD:]
    v_ref[0] = side_by_side(columns(2))
    g_ref[0] = jax.nn.sigmoid(columns(3) + gs_ref[own, :])


def matrix(second):
    return pl.BlockSpec((1, HD, HD), lambda i: (int(second), 0, 0))


def project(crossed, x, vectors, matrices):
    whole = pl.BlockSpec(memory_space=pltpu.VMEM)
    row_spec = pl.BlockSpec((1, TOKENS, HD), lambda i: (i, 0, 0))
    head_spec = pl.BlockSpec((1, HEADS, TOKENS, HD), lambda i: (i, 0, 0, 0))
    scratch = [
        pltpu.VMEM((2 * HD, 4 * HD), BF16),
        pltpu.VMEM((HD, 4 * HD), BF16),
        pltpu.VMEM((2, 2 * HD, HEADS * HD), BF16),
    ]
    if crossed:
        scratch.append(pltpu.VMEM((TOKENS, HD), F32))
    return pl.pallas_call(
        functools.partial(project_kernel, crossed),
        grid=(ROWS,),
        in_specs=[whole if crossed else row_spec] + [whole] * 3 + [matrix(crossed)] * 4,
        out_specs=[
            head_spec, head_spec, pl.BlockSpec((1, TOKENS, 2 * HD), lambda i: (i, 0, 0)), row_spec,
        ],
        out_shape=[
            jax.ShapeDtypeStruct((ROWS, HEADS, TOKENS, HD), BF16),
            jax.ShapeDtypeStruct((ROWS, HEADS, TOKENS, HD), BF16),
            jax.ShapeDtypeStruct((ROWS, TOKENS, 2 * HD), BF16),
            jax.ShapeDtypeStruct((ROWS, TOKENS, HD), F32),
        ],
        scratch_shapes=scratch,
        compiler_params=pltpu.CompilerParams(
            vmem_limit_bytes=VMEM, dimension_semantics=("arbitrary",)
        ),
        cost_estimate=pl.CostEstimate(
            flops=10**10, bytes_accessed=17 * 10**6, transcendentals=10**6
        ),
    )(x, *vectors, *matrices)


def build_plane(scalar_ref, piece_refs, plane_ref, turned):
    my_x, my_z, core, real = scalar_ref[0], scalar_ref[2], scalar_ref[3], scalar_ref[4]
    limit = ((real + 255) // 256) * 256

    def one_group(group, _):
        x_hi, z, x_lo = group % 2, (group // 2) % 4, group // 8
        behind_x, behind_z = (my_x - (x_hi * 2 + x_lo)) & 3, (my_z - z) & 3
        rows = pl.ds(pl.multiple_of(group * 48, 16), 48)

        def one_half(own):
            half = core if own else 1 - core
            lanes = pl.ds(pl.multiple_of(half * 384, 128), 384)
            if turned:
                key = lax.broadcasted_iota(jnp.int32, (48, 384), 0) + group * 48
                needed = group * 48 < limit
            else:
                key = lax.broadcasted_iota(jnp.int32, (48, 384), 1) + half * 384
                needed = half * 384 < limit

            @pl.when(needed)
            def _():
                for head in range(HEADS):
                    if head < 2:
                        at = behind_z * 4 + behind_x
                    else:
                        at = behind_x * 4 + behind_z
                    values = piece_refs[head // 2 * 2 + (0 if own else 1)][at, head % 2]
                    plane_ref[head, rows, lanes] = jnp.where(
                        key < real, values.astype(F32) * LOG2E, NEGATIVE
                    )

        one_half(True)
        one_half(False)
        return 0

    lax.fori_loop(0, 16, one_group, 0)

    def turn(head, _):
        for a in range(6):

            @pl.when(a * 128 < limit)
            def _():
                for b in range(a, 6):
                    aa, bb = slice(a * 128, a * 128 + 128), slice(b * 128, b * 128 + 128)
                    upper = plane_ref[head, aa, bb]
                    lower = plane_ref[head, bb, aa]
                    plane_ref[head, aa, bb] = lower.T
                    if a != b:
                        plane_ref[head, bb, aa] = upper.T
        return 0

    if turned:
        lax.fori_loop(0, HEADS, turn, 0)


def attend(keys, q_ref, k_ref, v_ref, plane_ref, mixed_ref):
    group = lane_group()
    value = total = None
    for head in range(HEADS):
        scores = dot(q_ref[0, head], k_ref[0, head, :keys, :], NT) + plane_ref[head, :, :keys]
        highest = jnp.max(scores, axis=-1, keepdims=True)
        weights = jnp.exp2(scores - highest).astype(BF16)
        weight = jnp.sum(weights.astype(F32), axis=-1, keepdims=True)
        mixed = dot(weights, v_ref[0, :keys, :])
        mixed = mixed[:, :HD] + mixed[:, HD:]
        weight = jnp.broadcast_to(weight, mixed.shape)
        value = mixed if head == 0 else jnp.where(group == head, mixed, value)
        total = weight if head == 0 else jnp.where(group == head, weight, total)
    mixed_ref[...] = value / total


def attend_kernel(turned, scalar_ref, q_ref, k_ref, v_ref, g_ref, wo_ref, *rest):
    piece_refs, rest = rest[:4], rest[4:]
    step = pl.program_id(0)
    if turned:
        crossed_ref, plane_ref, mixed_ref = rest
    else:
        x_ref, gain_ref, shift_ref, nbias_ref = rest[:4]
        first_ref, crossed_ref, kept_ref, sent_ref, plane_ref, mixed_ref, rows_ref = rest[4:]

    @pl.when(step == 0)
    def _():
        build_plane(scalar_ref, piece_refs, plane_ref, turned)

    real = scalar_ref[4]
    for keys in (256, 512, 768):

        @pl.when((real > keys - 256) & (real <= keys))
        def _():
            attend(keys, q_ref, k_ref, v_ref, plane_ref, mixed_ref)

    update = dot_split(side_by_side(g_ref[0] * mixed_ref[...]), *twice(wo_ref[0]))
    if turned:
        mixed_ref[...] = update
        for row in range(ROWS):
            crossed_ref[pl.ds(row * ROWS + step, DEVICES, stride=PADDED), :] = mixed_ref[
                pl.ds(row, DEVICES, stride=ROWS), :
            ]
    else:
        first = x_ref[0] + update
        first_ref[0] = first
        standard = standardize(first)
        mixed_ref[...] = encode(standard)
        for column in range(ROWS):
            crossed_ref[pl.ds(step * ROWS + column, DEVICES, stride=PADDED), :] = mixed_ref[
                pl.ds(column, DEVICES, stride=ROWS), :
            ]
        normed = standard * gain_ref[1:2, :] + shift_ref[1:2, :]
        bias = dot3(split(nbias_ref[1]), split(normed), NT)
        for row in range(ROWS):

            @pl.when(step == row)
            def _():
                for half in range(2):
                    at = half * 24 + row * 4
                    rows_ref[at : at + 4, :] = bias[:, half * 384 : (half + 1) * 384]

        @pl.when(step == ROWS - 1)
        def _():
            hand_over(scalar_ref, rows_ref, kept_ref, sent_ref)


def run_pass(turned, scalars, projected, w_o, pieces, x=None, extra=()):
    whole = pl.BlockSpec(memory_space=pltpu.VMEM)
    row_spec = pl.BlockSpec((1, TOKENS, HD), lambda i: (i, 0, 0))
    head_spec = pl.BlockSpec((1, HEADS, TOKENS, HD), lambda i: (i, 0, 0, 0))
    in_specs = [pl.BlockSpec(memory_space=pltpu.SMEM), head_spec, head_spec]
    in_specs += [pl.BlockSpec((1, TOKENS, 2 * HD), lambda i: (i, 0, 0)), row_spec]
    in_specs += [matrix(turned)] + [whole] * 4
    out_shape = [jax.ShapeDtypeStruct((DEVICES * PADDED, HD), F32)]
    out_specs = [pl.BlockSpec((DEVICES * PADDED, HD), lambda i: (0, 0))]
    scratch = [pltpu.VMEM((HEADS, TOKENS, TOKENS), F32), pltpu.VMEM((TOKENS, HD), F32)]
    args = [scalars, *projected, w_o, *pieces]
    if not turned:
        in_specs += [row_spec] + [whole] * 3
        args += [x, *extra]
        out_shape = [jax.ShapeDtypeStruct((ROWS, TOKENS, HD), F32)] + out_shape
        out_shape += [jax.ShapeDtypeStruct((24, 384), BF16)] * 2
        out_specs = [row_spec] + out_specs + [pl.BlockSpec((24, 384), lambda i: (0, 0))] * 2
        scratch.append(pltpu.VMEM((48, 384), F32))
    return pl.pallas_call(
        functools.partial(attend_kernel, turned),
        grid=(ROWS,),
        in_specs=in_specs,
        out_specs=out_specs,
        out_shape=out_shape,
        scratch_shapes=scratch,
        compiler_params=pltpu.CompilerParams(
            vmem_limit_bytes=VMEM, dimension_semantics=("arbitrary",)
        ),
        cost_estimate=pl.CostEstimate(
            flops=2 * 10**10, bytes_accessed=2 * 10**7, transcendentals=14 * 10**6
        ),
    )(*args)


def final_kernel(first_ref, update_ref, out_ref, row_ref):
    step = pl.program_id(0)
    for column in range(ROWS):
        row_ref[pl.ds(column, DEVICES, stride=ROWS), :] = update_ref[
            pl.ds(step * ROWS + column, DEVICES, stride=PADDED), :
        ]
    out_ref[0] = first_ref[0] + row_ref[...]


def add_crossed(first, update):
    row_spec = pl.BlockSpec((1, TOKENS, HD), lambda i: (i, 0, 0))
    return pl.pallas_call(
        final_kernel,
        grid=(ROWS,),
        in_specs=[row_spec, pl.BlockSpec(memory_space=pltpu.VMEM)],
        out_specs=row_spec,
        out_shape=jax.ShapeDtypeStruct((ROWS, TOKENS, HD), F32),
        scratch_shapes=[pltpu.VMEM((TOKENS, HD), F32)],
        compiler_params=pltpu.CompilerParams(
            vmem_limit_bytes=VMEM, dimension_semantics=("arbitrary",)
        ),
        cost_estimate=pl.CostEstimate(flops=10**6, bytes_accessed=8 * 10**6, transcendentals=0),
    )(first, update)


def cross(values):
    return lax.all_to_all(values, AXES, split_axis=0, concat_axis=0, tiled=True)


def on_device(
    pair_tensor,
    token_mask,
    ln_gain,
    ln_shift,
    w_query,
    w_key,
    w_value,
    w_bias,
    w_gate,
    gate_shift,
    w_out,
):
    row, col = lax.axis_index("row"), lax.axis_index("col")
    place = [(col // 8) * 2 + row // 4, (col // 2) % 4, row % 4, col % 2]
    place = jnp.stack([jnp.int32(p) for p in place])
    vectors, matrices = (ln_gain, ln_shift, gate_shift), (w_query, w_key, w_value, w_gate)

    start = first_bias(place, pair_tensor, ln_gain, ln_shift, w_bias)
    planes, projected = gather_plane(
        place, *start, pair_tensor, lambda cells: project(False, cells, vectors, matrices)
    )
    scalars = jnp.concatenate([place, jnp.sum(token_mask, dtype=jnp.int32, keepdims=True)])
    first, codes, *end = run_pass(
        False, scalars, projected, w_out, planes, pair_tensor, (ln_gain, ln_shift, w_bias)
    )
    codes = cross(codes.astype(jnp.int16))
    planes, projected = gather_plane(
        place, *end, codes, lambda held: project(True, held.astype(F32), vectors, matrices)
    )
    (update,) = run_pass(True, scalars, projected, w_out, planes)
    return add_crossed(first, cross(update.astype(jnp.float16)).astype(F32))


def solution(mesh):
    placed = (P(AXES, None, None), P(), P(), P(), P(), P(), P(), P(), P(), P(), P())
    return jax.shard_map(
        on_device,
        mesh=mesh,
        in_specs=placed,
        out_specs=P(AXES, None, None),
        check_vma=False,
    )
```

```python
import functools

import jax
import jax.numpy as jnp
import numpy as np
from jax import lax
from jax.experimental import pallas as pl
from jax.experimental.pallas import tpu as pltpu
from jax.sharding import PartitionSpec as P

HEADS = 4
HEAD_DIM = 32
HD = 128
TOKENS = 768
ROWS = 6
DEVICES = 128
PADDED = 40
EPSILON = 1e-05
NEGATIVE = -1e30
LOG2E = 1.4426950408889634
CURVE = 4.0
CODE_STEP = float(np.log(1 + CURVE * 11.32) / 32767)
AXES = ("row", "col")
MIB = 1024 * 1024
F32, BF16 = jnp.float32, jnp.bfloat16
NT = (((1,), (1,)), ((), ()))
NN = (((1,), (0,)), ((), ()))


def coords(device):
    row, col = divmod(device, 16)
    x_lo, z = divmod(row, 4)
    x_hi, rest = divmod(col, 8)
    y, core = divmod(rest, 2)
    return [x_hi * 2 + x_lo, y, z, core]


def device_at(x, y, z, core):
    return ((x % 2) * 4 + z) * 16 + (x // 2) * 8 + y * 2 + core


def shifted(values, axis, step):
    pairs = []
    for source in range(DEVICES):
        place = coords(source)
        place[axis] = (place[axis] + step) % (2 if axis == 3 else 4)
        pairs.append((source, device_at(*place)))
    return lax.ppermute(values, AXES, pairs)


def ring(block, axis):
    return jnp.concatenate(
        [block, shifted(block, axis, 1), shifted(block, axis, 2), shifted(block, axis, -1)], 0
    )


def merge_kernel(scalar_ref, *refs):
    to = lax.broadcasted_iota(jnp.int32, (192, 192), 0)
    of = lax.broadcasted_iota(jnp.int32, (192, 192), 1)
    head, y, core, row = to // 48, (to // 12) % 4, (to // 6) % 2, to % 6
    behind = (scalar_ref[1] - y) & 3
    source = (behind * 2 + (core ^ scalar_ref[3])) * 24 + row * 4 + head
    order = jnp.where(of == source, 1.0, 0.0).astype(BF16)
    slots = jnp.concatenate([ref[...] for ref in refs[:4]], axis=0)
    ordered = dot(order, slots).astype(BF16)
    for head_at in range(HEADS):
        refs[4 + head_at // 2][head_at % 2] = ordered[head_at * 48 : (head_at + 1) * 48]


def merge(scalars, slots):
    vmem = pl.BlockSpec(memory_space=pltpu.VMEM)
    return pl.pallas_call(
        merge_kernel,
        in_specs=[pl.BlockSpec(memory_space=pltpu.SMEM)] + [vmem] * 4,
        out_shape=[jax.ShapeDtypeStruct((2, 48, 384), BF16)] * 2,
        compiler_params=pltpu.CompilerParams(vmem_limit_bytes=8 * MIB),
        cost_estimate=pl.CostEstimate(flops=10**7, bytes_accessed=3 * 10**5, transcendentals=0),
    )(scalars, *slots)


def gather_plane(place, kept, sent, beside, work, crossing=False):
    block = jnp.concatenate([kept, shifted(sent, 3, 1)], axis=0)
    slots = [block] + [shifted(block, 1, step) for step in (1, 2, -1)]
    if crossing:
        *slots, beside = lax.optimization_barrier((*slots, beside))
        beside = cross(beside)
    blocks = [ring(pair[None], axis) for pair, axis in zip(merge(place, slots), (0, 2))]
    blocks, beside = lax.optimization_barrier((blocks, beside))
    blocks = [ring(block, axis) for block, axis in zip(blocks, (2, 0))]
    blocks, done = lax.optimization_barrier((blocks, work(beside)))
    pieces = []
    for block in blocks:
        pieces += [block, shifted(block, 3, 1)]
    return pieces, done


def split(values):
    high = values.astype(BF16)
    return high, (values - high.astype(F32)).astype(BF16)


def dot(a, b, dims=NN):
    return lax.dot_general(a, b, dims, preferred_element_type=F32)


def dot3(a, b, dims=NN):
    (a_high, a_low), (b_high, b_low) = a, b
    return dot(a_high, b_high, dims) + (dot(a_low, b_high, dims) + dot(a_high, b_low, dims))


def dot_split(a, b_twice, b_low):
    return dot(a, b_twice) + dot(a[:, :HD], b_low)


def side_by_side(values):
    return jnp.concatenate(split(values), axis=1)


def twice(weight):
    high, low = split(weight)
    return jnp.concatenate([high, high], axis=0), low


def standardize(values):
    mean = jnp.full((2 * HD, HD), 1.0 / HD, BF16)
    centred = values - dot(side_by_side(values), mean)
    spread = dot(side_by_side(centred * centred), mean)
    return centred * lax.rsqrt(spread + EPSILON)


def normalize(values, gain, shift):
    return standardize(values) * gain + shift


def encode(values):
    size = jnp.floor(jnp.log(1.0 + CURVE * jnp.abs(values)) * (1 / CODE_STEP) + 0.5)
    return jnp.where(values < 0, -size, size)


def decode(codes):
    size = (jnp.exp(jnp.abs(codes) * CODE_STEP) - 1.0) * (1 / CURVE)
    return jnp.where(codes < 0, -size, size)


def put_bias(normed, w_bias, rows_ref, step, count):
    bias = dot3(split(w_bias), split(normed), NT)
    for row in range(count):

        @pl.when(step == row)
        def _():
            for half in range(2):
                at = half * 24 + row * 4
                rows_ref[at : at + 4, :] = bias[:, half * 384 : (half + 1) * 384]


def hand_over(scalar_ref, rows_ref, kept_ref, sent_ref):
    first, second = rows_ref[:24, :].astype(BF16), rows_ref[24:, :].astype(BF16)
    kept_ref[...] = jnp.where(scalar_ref[3] == 0, first, second)
    sent_ref[...] = jnp.where(scalar_ref[3] == 0, second, first)


def bias_kernel(scalar_ref, x_ref, gain_ref, shift_ref, w_ref, kept_ref, sent_ref, rows_ref):
    step = pl.program_id(0)
    normed = normalize(x_ref[0], gain_ref[0:1, :], shift_ref[0:1, :])
    put_bias(normed, w_ref[0], rows_ref, step, ROWS)

    @pl.when(step == ROWS - 1)
    def _():
        hand_over(scalar_ref, rows_ref, kept_ref, sent_ref)


def small(*shape):
    return pl.BlockSpec(shape, lambda i: (0,) * len(shape))


def first_bias(scalars, x, gain, shift, w_bias):
    return pl.pallas_call(
        bias_kernel,
        grid=(ROWS,),
        in_specs=[
            pl.BlockSpec(memory_space=pltpu.SMEM),
            pl.BlockSpec((1, TOKENS, HD), lambda i: (i, 0, 0)),
            small(2, HD),
            small(2, HD),
            small(2, HEADS, HD),
        ],
        out_specs=[small(24, 384)] * 2,
        out_shape=[jax.ShapeDtypeStruct((24, 384), BF16)] * 2,
        scratch_shapes=[pltpu.VMEM((48, 384), F32)],
        compiler_params=pltpu.CompilerParams(
            vmem_limit_bytes=24 * MIB, dimension_semantics=("arbitrary",)
        ),
        cost_estimate=pl.CostEstimate(flops=10**8, bytes_accessed=2 * 10**6, transcendentals=0),
    )(scalars, x, gain, shift, w_bias)


def lane_group():
    return lax.broadcasted_iota(jnp.int32, (1, HD), 1) // HEAD_DIM


def spreader(source_of):
    row = lax.broadcasted_iota(jnp.int32, (2 * HD, HEADS * HD), 0)
    column = lax.broadcasted_iota(jnp.int32, (2 * HD, HEADS * HD), 1)
    head, group, d = column // HD, (column // HEAD_DIM) % 4, column % HEAD_DIM
    part = source_of(head, group)
    hit = (part >= 0) & (row == part * HD + head * HEAD_DIM + d)
    return jnp.where(hit, 1.0, 0.0).astype(BF16)


def prepare_weights(weights, w_twice_ref, w_low_ref, spread_ref):
    for at, weight in enumerate(weights):
        high, low = twice(weight)
        w_twice_ref[:, at * HD : (at + 1) * HD] = high
        w_low_ref[:, at * HD : (at + 1) * HD] = low
    spread_ref[0] = spreader(lambda head, group: group % 2)
    spread_ref[1] = spreader(lambda head, group: group // 2)


def project_kernel(
    crossed, x_ref, gain_ref, shift_ref, gs_ref, wq_ref, wk_ref, wv_ref, wg_ref, q_ref, k_ref, v_ref, g_ref,
    w_twice_ref, w_low_ref, spread_ref, *rest,
):
    step = pl.program_id(0)

    @pl.when(step == 0)
    def _():
        weights = [wq_ref[0] * (HEAD_DIM**-0.5 * LOG2E), wk_ref[0], wv_ref[0], wg_ref[0]]
        prepare_weights(weights, w_twice_ref, w_low_ref, spread_ref)

    if crossed:
        for row in range(ROWS):
            rest[0][pl.ds(row, DEVICES, stride=ROWS), :] = x_ref[
                pl.ds(row * ROWS + step, DEVICES, stride=PADDED), :
            ]
        standard = decode(rest[0][...])
    else:
        standard = standardize(x_ref[0])
    own = slice(int(crossed), int(crossed) + 1)
    cells = side_by_side(standard * gain_ref[own, :] + shift_ref[own, :])

    def columns(at):
        cut = slice(at * HD, (at + 1) * HD)
        return dot_split(cells, w_twice_ref[:, cut], w_low_ref[:, cut])

    for at, ref in enumerate((q_ref, k_ref)):
        parts = side_by_side(columns(at))
        for pair in range(2):
            cut = slice(pair * 2 * HD, (pair + 1) * 2 * HD)
            spread = dot(parts, spread_ref[at, :, cut]).astype(BF16)
            ref[0, 2 * pair] = spread[:, :HD]
            ref[0, 2 * pair + 1] = spread[:, HD:]
    v_ref[0] = side_by_side(columns(2))
    g_ref[0] = jax.nn.sigmoid(columns(3) + gs_ref[own, :])


def matrix(second):
    return pl.BlockSpec((1, HD, HD), lambda i: (int(second), 0, 0))


def project(crossed, x, vectors, matrices):
    whole = pl.BlockSpec(memory_space=pltpu.VMEM)
    row_spec = pl.BlockSpec((1, TOKENS, HD), lambda i: (i, 0, 0))
    head_spec = pl.BlockSpec((1, HEADS, TOKENS, HD), lambda i: (i, 0, 0, 0))
    scratch = [
        pltpu.VMEM((2 * HD, 4 * HD), BF16),
        pltpu.VMEM((HD, 4 * HD), BF16),
        pltpu.VMEM((2, 2 * HD, HEADS * HD), BF16),
    ]
    if crossed:
        scratch.append(pltpu.VMEM((TOKENS, HD), F32))
    return pl.pallas_call(
        functools.partial(project_kernel, crossed),
        grid=(ROWS,),
        in_specs=[whole if crossed else row_spec] + [small(2, HD)] * 3 + [matrix(crossed)] * 4,
        out_specs=[
            head_spec, head_spec, pl.BlockSpec((1, TOKENS, 2 * HD), lambda i: (i, 0, 0)), row_spec,
        ],
        out_shape=[
            jax.ShapeDtypeStruct((ROWS, HEADS, TOKENS, HD), BF16),
            jax.ShapeDtypeStruct((ROWS, HEADS, TOKENS, HD), BF16),
            jax.ShapeDtypeStruct((ROWS, TOKENS, 2 * HD), BF16),
            jax.ShapeDtypeStruct((ROWS, TOKENS, HD), F32),
        ],
        scratch_shapes=scratch,
        compiler_params=pltpu.CompilerParams(
            vmem_limit_bytes=24 * MIB, dimension_semantics=("arbitrary",)
        ),
        cost_estimate=pl.CostEstimate(
            flops=10**10, bytes_accessed=17 * 10**6, transcendentals=10**6
        ),
    )(x, *vectors, *matrices)


def build_plane(scalar_ref, piece_refs, plane_ref, flat_ref, turned):
    my_x, my_z, core, real = scalar_ref[0], scalar_ref[2], scalar_ref[3], scalar_ref[4]
    limit = ((real + 255) // 256) * 256

    def one_group(group, _):
        x_hi, z, x_lo = group % 2, (group // 2) % 4, group // 8
        behind_x, behind_z = (my_x - (x_hi * 2 + x_lo)) & 3, (my_z - z) & 3
        rows = pl.ds(pl.multiple_of(group * 48, 16), 48)

        def one_half(own):
            half = core if own else 1 - core
            lanes = pl.ds(pl.multiple_of(half * 384, 128), 384)
            needed = group * 48 < limit if turned else half * 384 < limit

            @pl.when(needed)
            def _():
                for head in range(HEADS):
                    if head < 2:
                        at = behind_z * 4 + behind_x
                    else:
                        at = behind_x * 4 + behind_z
                    values = piece_refs[head // 2 * 2 + (0 if own else 1)][at, head % 2]
                    if turned:
                        flat_ref[head, rows, lanes] = values
                    else:
                        key = lax.broadcasted_iota(jnp.int32, (48, 384), 1) + half * 384
                        plane_ref[head, rows, lanes] = jnp.where(
                            key < real, values.astype(F32) * LOG2E, NEGATIVE
                        )

        one_half(True)
        one_half(False)
        return 0

    lax.fori_loop(0, 16, one_group, 0)

    def turn(head, _):
        for block in range(6):
            keys = slice(block * 128, block * 128 + 128)

            @pl.when(block * 128 < limit)
            def _():
                live = lax.broadcasted_iota(jnp.int32, (128, 128), 1) + block * 128 < real
                for other in range(6):
                    rows = slice(other * 128, other * 128 + 128)
                    values = flat_ref[head, keys, rows].T.astype(F32) * LOG2E
                    plane_ref[head, rows, keys] = jnp.where(live, values, NEGATIVE)
        return 0

    if turned:
        lax.fori_loop(0, HEADS, turn, 0)


def attend(keys, q_ref, k_ref, v_ref, plane_ref, mixed_ref):
    group = lane_group()
    value = total = None
    for head in range(HEADS):
        scores = dot(q_ref[0, head], k_ref[0, head, :keys, :], NT) + plane_ref[head, :, :keys]
        highest = jnp.max(scores, axis=-1, keepdims=True)
        weights = jnp.exp2(scores - highest).astype(BF16)
        weight = jnp.sum(weights.astype(F32), axis=-1, keepdims=True)
        mixed = dot(weights, v_ref[0, :keys, :])
        mixed = mixed[:, :HD] + mixed[:, HD:]
        weight = jnp.broadcast_to(weight, mixed.shape)
        value = mixed if head == 0 else jnp.where(group == head, mixed, value)
        total = weight if head == 0 else jnp.where(group == head, weight, total)
    mixed_ref[...] = value / total


def attend_kernel(turned, scalar_ref, q_ref, k_ref, v_ref, g_ref, wo_ref, *rest):
    piece_refs, rest = rest[:4], rest[4:]
    step = pl.program_id(0)
    if turned:
        crossed_ref, plane_ref, mixed_ref, flat_ref = rest
    else:
        x_ref, gain_ref, shift_ref, nbias_ref = rest[:4]
        first_ref, crossed_ref, kept_ref, sent_ref = rest[4:8]
        plane_ref, mixed_ref, rows_ref, wide_ref = rest[8:]

    @pl.when(step == 0)
    def _():
        build_plane(scalar_ref, piece_refs, plane_ref, flat_ref if turned else None, turned)
        if not turned:
            wide_ref[...] = jnp.zeros_like(wide_ref)

    real = scalar_ref[4]
    for keys in (256, 512, 768):

        @pl.when((real > keys - 256) & (real <= keys))
        def _():
            attend(keys, q_ref, k_ref, v_ref, plane_ref, mixed_ref)

    update = dot_split(side_by_side(g_ref[0] * mixed_ref[...]), *twice(wo_ref[0]))
    if turned:
        mixed_ref[...] = update
        for row in range(ROWS):
            crossed_ref[pl.ds(row * ROWS + step, DEVICES, stride=PADDED), :] = mixed_ref[
                pl.ds(row, DEVICES, stride=ROWS), :
            ]
    else:
        first = x_ref[0] + update
        first_ref[0] = first
        standard = standardize(first)
        mixed_ref[...] = encode(standard)
        for column in range(ROWS):
            wide_ref[pl.ds(step * ROWS + column, DEVICES, stride=PADDED), :] = mixed_ref[
                pl.ds(column, DEVICES, stride=ROWS), :
            ]
        normed = standard * gain_ref[1:2, :] + shift_ref[1:2, :]
        put_bias(normed, nbias_ref[1], rows_ref, step, ROWS)

        @pl.when(step == ROWS - 1)
        def _():
            crossed_ref[...] = wide_ref[...].astype(jnp.int32).astype(jnp.int16)
            hand_over(scalar_ref, rows_ref, kept_ref, sent_ref)


def run_pass(turned, scalars, projected, w_o, pieces, x=None, extra=()):
    whole = pl.BlockSpec(memory_space=pltpu.VMEM)
    row_spec = pl.BlockSpec((1, TOKENS, HD), lambda i: (i, 0, 0))
    head_spec = pl.BlockSpec((1, HEADS, TOKENS, HD), lambda i: (i, 0, 0, 0))
    in_specs = [pl.BlockSpec(memory_space=pltpu.SMEM), head_spec, head_spec]
    in_specs += [pl.BlockSpec((1, TOKENS, 2 * HD), lambda i: (i, 0, 0)), row_spec]
    in_specs += [matrix(turned)] + [whole] * 4
    out_shape = [jax.ShapeDtypeStruct((DEVICES * PADDED, HD), F32 if turned else jnp.int16)]
    out_specs = [pl.BlockSpec((DEVICES * PADDED, HD), lambda i: (0, 0))]
    scratch = [pltpu.VMEM((HEADS, TOKENS, TOKENS), F32), pltpu.VMEM((TOKENS, HD), F32)]
    if turned:
        scratch.append(pltpu.VMEM((HEADS, TOKENS, TOKENS), BF16))
    args = [scalars, *projected, w_o, *pieces]
    if not turned:
        in_specs += [row_spec, small(2, HD), small(2, HD), small(2, HEADS, HD)]
        args += [x, *extra]
        out_shape = [jax.ShapeDtypeStruct((ROWS, TOKENS, HD), F32)] + out_shape
        out_shape += [jax.ShapeDtypeStruct((24, 384), BF16)] * 2
        out_specs = [row_spec] + out_specs + [pl.BlockSpec((24, 384), lambda i: (0, 0))] * 2
        scratch += [pltpu.VMEM((48, 384), F32), pltpu.VMEM((DEVICES * PADDED, HD), F32)]
    return pl.pallas_call(
        functools.partial(attend_kernel, turned),
        grid=(ROWS,),
        in_specs=in_specs,
        out_specs=out_specs,
        out_shape=out_shape,
        scratch_shapes=scratch,
        compiler_params=pltpu.CompilerParams(
            vmem_limit_bytes=26 * MIB, dimension_semantics=("arbitrary",)
        ),
        cost_estimate=pl.CostEstimate(
            flops=2 * 10**10, bytes_accessed=2 * 10**7, transcendentals=14 * 10**6
        ),
    )(*args)


def final_kernel(first_ref, update_ref, out_ref, row_ref):
    step = pl.program_id(0)
    for column in range(ROWS):
        row_ref[pl.ds(column, DEVICES, stride=ROWS), :] = update_ref[
            pl.ds(step * ROWS + column, DEVICES, stride=PADDED), :
        ]
    out_ref[0] = first_ref[0] + row_ref[...]


def add_crossed(first, update):
    row_spec = pl.BlockSpec((1, TOKENS, HD), lambda i: (i, 0, 0))
    return pl.pallas_call(
        final_kernel,
        grid=(ROWS,),
        in_specs=[row_spec, pl.BlockSpec(memory_space=pltpu.VMEM)],
        out_specs=row_spec,
        out_shape=jax.ShapeDtypeStruct((ROWS, TOKENS, HD), F32),
        scratch_shapes=[pltpu.VMEM((TOKENS, HD), F32)],
        compiler_params=pltpu.CompilerParams(
            vmem_limit_bytes=16 * MIB, dimension_semantics=("arbitrary",)
        ),
        cost_estimate=pl.CostEstimate(flops=10**6, bytes_accessed=8 * 10**6, transcendentals=0),
    )(first, update)


def cross(values):
    return lax.all_to_all(values, AXES, split_axis=0, concat_axis=0, tiled=True)


def on_device(
    pair_tensor,
    token_mask,
    ln_gain,
    ln_shift,
    w_query,
    w_key,
    w_value,
    w_bias,
    w_gate,
    gate_shift,
    w_out,
):
    row, col = lax.axis_index("row"), lax.axis_index("col")
    place = [(col // 8) * 2 + row // 4, (col // 2) % 4, row % 4, col % 2]
    place = jnp.stack([jnp.int32(p) for p in place])
    vectors, matrices = (ln_gain, ln_shift, gate_shift), (w_query, w_key, w_value, w_gate)

    start = first_bias(place, pair_tensor, ln_gain, ln_shift, w_bias)
    scalars = jnp.concatenate([place, jnp.sum(token_mask, dtype=jnp.int32, keepdims=True)])
    planes, (projected, scalars) = gather_plane(
        place, *start, (pair_tensor, scalars),
        lambda held: (project(False, held[0], vectors, matrices), held[1]),
    )
    first, codes, *end = run_pass(
        False, scalars, projected, w_out, planes, pair_tensor, (ln_gain, ln_shift, w_bias)
    )
    planes, projected = gather_plane(
        place, *end, codes, lambda held: project(True, held.astype(F32), vectors, matrices), True
    )
    (update,) = run_pass(True, scalars, projected, w_out, planes)
    return add_crossed(first, cross(update.astype(jnp.float16)).astype(F32))


def solution(mesh):
    placed = (P(AXES, None, None), P(), P(), P(), P(), P(), P(), P(), P(), P(), P())
    return jax.shard_map(
        on_device,
        mesh=mesh,
        in_specs=placed,
        out_specs=P(AXES, None, None),
        check_vma=False,
    )
```

```python
import functools

import jax
import jax.numpy as jnp
import numpy as np
from jax import lax
from jax.experimental import pallas as pl
from jax.experimental.pallas import tpu as pltpu
from jax.sharding import PartitionSpec as P

HEADS = 4
HEAD_DIM = 32
HD = 128
TOKENS = 768
ROWS = 6
DEVICES = 128
PADDED = 40
EPSILON = 1e-05
NEGATIVE = -1e30
LOG2E = 1.4426950408889634
CURVE = 4.0
CODE_STEP = float(np.log(1 + CURVE * 11.32) / 32767)
AXES = ("row", "col")
MIB = 1024 * 1024
F32, BF16 = jnp.float32, jnp.bfloat16
NT = (((1,), (1,)), ((), ()))
NN = (((1,), (0,)), ((), ()))


def coords(device):
    row, col = divmod(device, 16)
    x_lo, z = divmod(row, 4)
    x_hi, rest = divmod(col, 8)
    y, core = divmod(rest, 2)
    return [x_hi * 2 + x_lo, y, z, core]


def device_at(x, y, z, core):
    return ((x % 2) * 4 + z) * 16 + (x // 2) * 8 + y * 2 + core


def shifted(values, axes, step):
    pairs = []
    for source in range(DEVICES):
        place = coords(source)
        axis = axes[place[3]]
        place[axis] = (place[axis] + step) % (2 if axis == 3 else 4)
        pairs.append((source, device_at(*place)))
    return lax.ppermute(values, AXES, pairs)


def ring(block, axes):
    return jnp.concatenate(
        [block, shifted(block, axes, 1), shifted(block, axes, 2), shifted(block, axes, -1)], 0
    )


def merge_kernel(scalar_ref, *refs):
    to = lax.broadcasted_iota(jnp.int32, (192, 192), 0)
    of = lax.broadcasted_iota(jnp.int32, (192, 192), 1)
    head, half, y, core, row = to // 96, (to // 48) % 2, (to // 12) % 4, (to // 6) % 2, to % 6
    behind = (scalar_ref[1] - y) & 3
    source = (behind * 2 + (core ^ scalar_ref[3])) * 24 + half * 12 + row * 2 + head
    order = jnp.where(of == source, 1.0, 0.0).astype(BF16)
    slots = jnp.concatenate([ref[...] for ref in refs[:4]], axis=0)
    ordered = dot(order, slots).astype(BF16)
    for part in range(4):
        lanes = slice(part % 2 * 384, (part % 2 + 1) * 384)
        refs[4][0, part // 2, :, lanes] = ordered[part * 48 : (part + 1) * 48]


def merge(scalars, slots):
    vmem = pl.BlockSpec(memory_space=pltpu.VMEM)
    return pl.pallas_call(
        merge_kernel,
        in_specs=[pl.BlockSpec(memory_space=pltpu.SMEM)] + [vmem] * 4,
        out_shape=jax.ShapeDtypeStruct((1, 2, 48, TOKENS), BF16),
        compiler_params=pltpu.CompilerParams(vmem_limit_bytes=8 * MIB),
        cost_estimate=pl.CostEstimate(flops=10**7, bytes_accessed=3 * 10**5, transcendentals=0),
    )(scalars, *slots)


def gather_plane(place, kept, sent, beside, work, crossing=False):
    block = jnp.concatenate([kept, shifted(sent, (3, 3), 1)], axis=0)
    slots = [block] + [shifted(block, (1, 1), step) for step in (1, 2, -1)]
    if crossing:
        *slots, beside = lax.optimization_barrier((*slots, beside))
        beside = cross(beside)
    block = ring(merge(place, slots), (0, 2))
    block, beside = lax.optimization_barrier((block, beside))
    block = ring(block, (2, 0))
    block, done = lax.optimization_barrier((block, work(beside)))
    return [block, shifted(block, (3, 3), 1)], done


def split(values):
    high = values.astype(BF16)
    return high, (values - high.astype(F32)).astype(BF16)


def dot(a, b, dims=NN):
    return lax.dot_general(a, b, dims, preferred_element_type=F32)


def dot3(a, b, dims=NN):
    (a_high, a_low), (b_high, b_low) = a, b
    return dot(a_high, b_high, dims) + (dot(a_low, b_high, dims) + dot(a_high, b_low, dims))


def dot_split(a, b_twice, b_low):
    return dot(a, b_twice) + dot(a[:, :HD], b_low)


def side_by_side(values):
    return jnp.concatenate(split(values), axis=1)


def twice(weight):
    high, low = split(weight)
    return jnp.concatenate([high, high], axis=0), low


def standardize(values):
    mean = jnp.full((2 * HD, HD), 1.0 / HD, BF16)
    centred = values - dot(side_by_side(values), mean)
    spread = dot(side_by_side(centred * centred), mean)
    return centred * lax.rsqrt(spread + EPSILON)


def normalize(values, gain, shift):
    return standardize(values) * gain + shift


def encode(values):
    size = jnp.floor(jnp.log(1.0 + CURVE * jnp.abs(values)) * (1 / CODE_STEP) + 0.5)
    return jnp.where(values < 0, -size, size)


def decode(codes):
    size = (jnp.exp(jnp.abs(codes) * CODE_STEP) - 1.0) * (1 / CURVE)
    return jnp.where(codes < 0, -size, size)


def put_bias(normed, w_bias, rows_ref, step, count):
    bias = dot3(split(w_bias), split(normed), NT)
    for row in range(count):

        @pl.when(step == row)
        def _():
            for part in range(4):
                pair, half = part // 2, part % 2
                at = pair * 24 + half * 12 + row * 2
                lanes = slice(half * 384, (half + 1) * 384)
                rows_ref[at : at + 2, :] = bias[pair * 2 : pair * 2 + 2, lanes]


def hand_over(scalar_ref, rows_ref, kept_ref, sent_ref):
    first, second = rows_ref[:24, :].astype(BF16), rows_ref[24:, :].astype(BF16)
    kept_ref[...] = jnp.where(scalar_ref[3] == 0, first, second)
    sent_ref[...] = jnp.where(scalar_ref[3] == 0, second, first)


def bias_kernel(scalar_ref, x_ref, gain_ref, shift_ref, w_ref, kept_ref, sent_ref, rows_ref):
    step = pl.program_id(0)
    normed = normalize(x_ref[0], gain_ref[0:1, :], shift_ref[0:1, :])
    put_bias(normed, w_ref[0], rows_ref, step, ROWS)

    @pl.when(step == ROWS - 1)
    def _():
        hand_over(scalar_ref, rows_ref, kept_ref, sent_ref)


def small(*shape):
    return pl.BlockSpec(shape, lambda i: (0,) * len(shape))


def first_bias(scalars, x, gain, shift, w_bias):
    return pl.pallas_call(
        bias_kernel,
        grid=(ROWS,),
        in_specs=[
            pl.BlockSpec(memory_space=pltpu.SMEM),
            pl.BlockSpec((1, TOKENS, HD), lambda i: (i, 0, 0)),
            small(2, HD),
            small(2, HD),
            small(2, HEADS, HD),
        ],
        out_specs=[small(24, 384)] * 2,
        out_shape=[jax.ShapeDtypeStruct((24, 384), BF16)] * 2,
        scratch_shapes=[pltpu.VMEM((48, 384), F32)],
        compiler_params=pltpu.CompilerParams(
            vmem_limit_bytes=24 * MIB, dimension_semantics=("arbitrary",)
        ),
        cost_estimate=pl.CostEstimate(flops=10**8, bytes_accessed=2 * 10**6, transcendentals=0),
    )(scalars, x, gain, shift, w_bias)


def lane_group():
    return lax.broadcasted_iota(jnp.int32, (1, HD), 1) // HEAD_DIM


def spreader(source_of):
    row = lax.broadcasted_iota(jnp.int32, (2 * HD, HEADS * HD), 0)
    column = lax.broadcasted_iota(jnp.int32, (2 * HD, HEADS * HD), 1)
    head, group, d = column // HD, (column // HEAD_DIM) % 4, column % HEAD_DIM
    part = source_of(head, group)
    hit = (part >= 0) & (row == part * HD + head * HEAD_DIM + d)
    return jnp.where(hit, 1.0, 0.0).astype(BF16)


def prepare_weights(weights, w_twice_ref, w_low_ref, spread_ref):
    for at, weight in enumerate(weights):
        high, low = twice(weight)
        w_twice_ref[:, at * HD : (at + 1) * HD] = high
        w_low_ref[:, at * HD : (at + 1) * HD] = low
    spread_ref[0] = spreader(lambda head, group: group % 2)
    spread_ref[1] = spreader(lambda head, group: group // 2)


def project_kernel(
    crossed, x_ref, gain_ref, shift_ref, gs_ref, wq_ref, wk_ref, wv_ref, wg_ref, q_ref, k_ref, v_ref, g_ref,
    w_twice_ref, w_low_ref, spread_ref, *rest,
):
    step = pl.program_id(0)

    @pl.when(step == 0)
    def _():
        weights = [wq_ref[0] * (HEAD_DIM**-0.5 * LOG2E), wk_ref[0], wv_ref[0], wg_ref[0]]
        prepare_weights(weights, w_twice_ref, w_low_ref, spread_ref)

    if crossed:
        for row in range(ROWS):
            rest[0][pl.ds(row, DEVICES, stride=ROWS), :] = x_ref[
                pl.ds(row * ROWS + step, DEVICES, stride=PADDED), :
            ]
        standard = decode(rest[0][...])
    else:
        standard = standardize(x_ref[0])
    own = slice(int(crossed), int(crossed) + 1)
    cells = side_by_side(standard * gain_ref[own, :] + shift_ref[own, :])

    def columns(at):
        cut = slice(at * HD, (at + 1) * HD)
        return dot_split(cells, w_twice_ref[:, cut], w_low_ref[:, cut])

    for at, ref in enumerate((q_ref, k_ref)):
        parts = side_by_side(columns(at))
        for pair in range(2):
            cut = slice(pair * 2 * HD, (pair + 1) * 2 * HD)
            spread = dot(parts, spread_ref[at, :, cut]).astype(BF16)
            ref[0, 2 * pair] = spread[:, :HD]
            ref[0, 2 * pair + 1] = spread[:, HD:]
    v_ref[0] = side_by_side(columns(2))
    g_ref[0] = jax.nn.sigmoid(columns(3) + gs_ref[own, :])


def matrix(second):
    return pl.BlockSpec((1, HD, HD), lambda i: (int(second), 0, 0))


def project(crossed, x, vectors, matrices):
    whole = pl.BlockSpec(memory_space=pltpu.VMEM)
    row_spec = pl.BlockSpec((1, TOKENS, HD), lambda i: (i, 0, 0))
    head_spec = pl.BlockSpec((1, HEADS, TOKENS, HD), lambda i: (i, 0, 0, 0))
    scratch = [
        pltpu.VMEM((2 * HD, 4 * HD), BF16),
        pltpu.VMEM((HD, 4 * HD), BF16),
        pltpu.VMEM((2, 2 * HD, HEADS * HD), BF16),
    ]
    if crossed:
        scratch.append(pltpu.VMEM((TOKENS, HD), F32))
    return pl.pallas_call(
        functools.partial(project_kernel, crossed),
        grid=(ROWS,),
        in_specs=[whole if crossed else row_spec] + [small(2, HD)] * 3 + [matrix(crossed)] * 4,
        out_specs=[
            head_spec, head_spec, pl.BlockSpec((1, TOKENS, 2 * HD), lambda i: (i, 0, 0)), row_spec,
        ],
        out_shape=[
            jax.ShapeDtypeStruct((ROWS, HEADS, TOKENS, HD), BF16),
            jax.ShapeDtypeStruct((ROWS, HEADS, TOKENS, HD), BF16),
            jax.ShapeDtypeStruct((ROWS, TOKENS, 2 * HD), BF16),
            jax.ShapeDtypeStruct((ROWS, TOKENS, HD), F32),
        ],
        scratch_shapes=scratch,
        compiler_params=pltpu.CompilerParams(
            vmem_limit_bytes=24 * MIB, dimension_semantics=("arbitrary",)
        ),
        cost_estimate=pl.CostEstimate(
            flops=10**10, bytes_accessed=17 * 10**6, transcendentals=10**6
        ),
    )(x, *vectors, *matrices)


def build_plane(scalar_ref, piece_refs, plane_ref, flat_ref, turned):
    my_x, my_z, core, real = scalar_ref[0], scalar_ref[2], scalar_ref[3], scalar_ref[4]
    limit = ((real + 255) // 256) * 256

    def one_group(group, _):
        x_hi, z, x_lo = group % 2, (group // 2) % 4, group // 8
        behind_x, behind_z = (my_x - (x_hi * 2 + x_lo)) & 3, (my_z - z) & 3
        rows = pl.ds(pl.multiple_of(group * 48, 16), 48)
        for ref, pair in zip(piece_refs, (core, 1 - core)):
            at = jnp.where(pair == 0, behind_z * 4 + behind_x, behind_x * 4 + behind_z)
            for half in range(2):
                lanes = slice(half * 384, (half + 1) * 384)

                @pl.when(group * 48 < limit if turned else half * 384 < limit)
                def _():
                    for odd in range(2):
                        values = ref[at, odd, :, lanes]
                        if turned:
                            flat_ref[pair * 2 + odd, rows, lanes] = values
                        else:
                            key = lax.broadcasted_iota(jnp.int32, (48, 384), 1) + half * 384
                            plane_ref[pair * 2 + odd, rows, lanes] = jnp.where(
                                key < real, values.astype(F32) * LOG2E, NEGATIVE
                            )
        return 0

    lax.fori_loop(0, 16, one_group, 0)

    def turn(head, _):
        for block in range(6):
            keys = slice(block * 128, block * 128 + 128)

            @pl.when(block * 128 < limit)
            def _():
                live = lax.broadcasted_iota(jnp.int32, (128, 128), 1) + block * 128 < real
                for other in range(6):
                    rows = slice(other * 128, other * 128 + 128)
                    values = flat_ref[head, keys, rows].T.astype(F32) * LOG2E
                    plane_ref[head, rows, keys] = jnp.where(live, values, NEGATIVE)
        return 0

    if turned:
        lax.fori_loop(0, HEADS, turn, 0)


def attend(keys, q_ref, k_ref, v_ref, plane_ref, mixed_ref):
    group = lane_group()
    value = total = None
    for head in range(HEADS):
        scores = dot(q_ref[0, head], k_ref[0, head, :keys, :], NT) + plane_ref[head, :, :keys]
        highest = jnp.max(scores, axis=-1, keepdims=True)
        weights = jnp.exp2(scores - highest).astype(BF16)
        weight = jnp.sum(weights.astype(F32), axis=-1, keepdims=True)
        mixed = dot(weights, v_ref[0, :keys, :])
        mixed = mixed[:, :HD] + mixed[:, HD:]
        weight = jnp.broadcast_to(weight, mixed.shape)
        value = mixed if head == 0 else jnp.where(group == head, mixed, value)
        total = weight if head == 0 else jnp.where(group == head, weight, total)
    mixed_ref[...] = value / total


def attend_kernel(turned, scalar_ref, q_ref, k_ref, v_ref, g_ref, wo_ref, *rest):
    piece_refs, rest = rest[:2], rest[2:]
    step = pl.program_id(0)
    if turned:
        crossed_ref, plane_ref, mixed_ref, flat_ref = rest
    else:
        x_ref, gain_ref, shift_ref, nbias_ref = rest[:4]
        first_ref, crossed_ref, kept_ref, sent_ref = rest[4:8]
        plane_ref, mixed_ref, rows_ref, wide_ref = rest[8:]

    @pl.when(step == 0)
    def _():
        build_plane(scalar_ref, piece_refs, plane_ref, flat_ref if turned else None, turned)
        if not turned:
            wide_ref[...] = jnp.zeros_like(wide_ref)

    real = scalar_ref[4]
    for keys in (256, 512, 768):

        @pl.when((real > keys - 256) & (real <= keys))
        def _():
            attend(keys, q_ref, k_ref, v_ref, plane_ref, mixed_ref)

    update = dot_split(side_by_side(g_ref[0] * mixed_ref[...]), *twice(wo_ref[0]))
    if turned:
        mixed_ref[...] = update
        for row in range(ROWS):
            crossed_ref[pl.ds(row * ROWS + step, DEVICES, stride=PADDED), :] = mixed_ref[
                pl.ds(row, DEVICES, stride=ROWS), :
            ]
    else:
        first = x_ref[0] + update
        first_ref[0] = first
        standard = standardize(first)
        mixed_ref[...] = encode(standard)
        for column in range(ROWS):
            wide_ref[pl.ds(step * ROWS + column, DEVICES, stride=PADDED), :] = mixed_ref[
                pl.ds(column, DEVICES, stride=ROWS), :
            ]
        normed = standard * gain_ref[1:2, :] + shift_ref[1:2, :]
        put_bias(normed, nbias_ref[1], rows_ref, step, ROWS)

        @pl.when(step == ROWS - 1)
        def _():
            crossed_ref[...] = wide_ref[...].astype(jnp.int32).astype(jnp.int16)
            hand_over(scalar_ref, rows_ref, kept_ref, sent_ref)


def run_pass(turned, scalars, projected, w_o, pieces, x=None, extra=()):
    whole = pl.BlockSpec(memory_space=pltpu.VMEM)
    row_spec = pl.BlockSpec((1, TOKENS, HD), lambda i: (i, 0, 0))
    head_spec = pl.BlockSpec((1, HEADS, TOKENS, HD), lambda i: (i, 0, 0, 0))
    in_specs = [pl.BlockSpec(memory_space=pltpu.SMEM), head_spec, head_spec]
    in_specs += [pl.BlockSpec((1, TOKENS, 2 * HD), lambda i: (i, 0, 0)), row_spec]
    in_specs += [matrix(turned)] + [whole] * 2
    out_shape = [jax.ShapeDtypeStruct((DEVICES * PADDED, HD), F32 if turned else jnp.int16)]
    out_specs = [pl.BlockSpec((DEVICES * PADDED, HD), lambda i: (0, 0))]
    scratch = [pltpu.VMEM((HEADS, TOKENS, TOKENS), F32), pltpu.VMEM((TOKENS, HD), F32)]
    if turned:
        scratch.append(pltpu.VMEM((HEADS, TOKENS, TOKENS), BF16))
    args = [scalars, *projected, w_o, *pieces]
    if not turned:
        in_specs += [row_spec, small(2, HD), small(2, HD), small(2, HEADS, HD)]
        args += [x, *extra]
        out_shape = [jax.ShapeDtypeStruct((ROWS, TOKENS, HD), F32)] + out_shape
        out_shape += [jax.ShapeDtypeStruct((24, 384), BF16)] * 2
        out_specs = [row_spec] + out_specs + [pl.BlockSpec((24, 384), lambda i: (0, 0))] * 2
        scratch += [pltpu.VMEM((48, 384), F32), pltpu.VMEM((DEVICES * PADDED, HD), F32)]
    return pl.pallas_call(
        functools.partial(attend_kernel, turned),
        grid=(ROWS,),
        in_specs=in_specs,
        out_specs=out_specs,
        out_shape=out_shape,
        scratch_shapes=scratch,
        compiler_params=pltpu.CompilerParams(
            vmem_limit_bytes=26 * MIB, dimension_semantics=("arbitrary",)
        ),
        cost_estimate=pl.CostEstimate(
            flops=2 * 10**10, bytes_accessed=2 * 10**7, transcendentals=14 * 10**6
        ),
    )(*args)


def final_kernel(first_ref, update_ref, out_ref, row_ref):
    step = pl.program_id(0)
    for column in range(ROWS):
        row_ref[pl.ds(column, DEVICES, stride=ROWS), :] = update_ref[
            pl.ds(step * ROWS + column, DEVICES, stride=PADDED), :
        ]
    out_ref[0] = first_ref[0] + row_ref[...]


def add_crossed(first, update):
    row_spec = pl.BlockSpec((1, TOKENS, HD), lambda i: (i, 0, 0))
    return pl.pallas_call(
        final_kernel,
        grid=(ROWS,),
        in_specs=[row_spec, pl.BlockSpec(memory_space=pltpu.VMEM)],
        out_specs=row_spec,
        out_shape=jax.ShapeDtypeStruct((ROWS, TOKENS, HD), F32),
        scratch_shapes=[pltpu.VMEM((TOKENS, HD), F32)],
        compiler_params=pltpu.CompilerParams(
            vmem_limit_bytes=16 * MIB, dimension_semantics=("arbitrary",)
        ),
        cost_estimate=pl.CostEstimate(flops=10**6, bytes_accessed=8 * 10**6, transcendentals=0),
    )(first, update)


def cross(values):
    return lax.all_to_all(values, AXES, split_axis=0, concat_axis=0, tiled=True)


def on_device(
    pair_tensor,
    token_mask,
    ln_gain,
    ln_shift,
    w_query,
    w_key,
    w_value,
    w_bias,
    w_gate,
    gate_shift,
    w_out,
):
    row, col = lax.axis_index("row"), lax.axis_index("col")
    place = [(col // 8) * 2 + row // 4, (col // 2) % 4, row % 4, col % 2]
    place = jnp.stack([jnp.int32(p) for p in place])
    vectors, matrices = (ln_gain, ln_shift, gate_shift), (w_query, w_key, w_value, w_gate)

    start = first_bias(place, pair_tensor, ln_gain, ln_shift, w_bias)
    scalars = jnp.concatenate([place, jnp.sum(token_mask, dtype=jnp.int32, keepdims=True)])
    planes, (projected, scalars) = gather_plane(
        place, *start, (pair_tensor, scalars),
        lambda held: (project(False, held[0], vectors, matrices), held[1]),
    )
    first, codes, *end = run_pass(
        False, scalars, projected, w_out, planes, pair_tensor, (ln_gain, ln_shift, w_bias)
    )
    planes, projected = gather_plane(
        place, *end, codes, lambda held: project(True, held.astype(F32), vectors, matrices), True
    )
    (update,) = run_pass(True, scalars, projected, w_out, planes)
    return add_crossed(first, cross(update.astype(jnp.float16)).astype(F32))


def solution(mesh):
    placed = (P(AXES, None, None), P(), P(), P(), P(), P(), P(), P(), P(), P(), P())
    return jax.shard_map(
        on_device,
        mesh=mesh,
        in_specs=placed,
        out_specs=P(AXES, None, None),
        check_vma=False,
    )
```

```python
import functools

import jax
import jax.numpy as jnp
import numpy as np
from jax import lax
from jax.experimental import pallas as pl
from jax.experimental.pallas import tpu as pltpu
from jax.sharding import PartitionSpec as P

HEADS = 4
HEAD_DIM = 32
HD = 128
TOKENS = 768
ROWS = 6
DEVICES = 128
PADDED = 40
EPSILON = 1e-05
NEGATIVE = -1e30
LOG2E = 1.4426950408889634
CURVE = 4.0
CODE_STEP = float(np.log(1 + CURVE * 11.32) / 32767)
AXES = ("row", "col")
MIB = 1024 * 1024
F32, BF16 = jnp.float32, jnp.bfloat16
NT = (((1,), (1,)), ((), ()))
NN = (((1,), (0,)), ((), ()))


def coords(device):
    row, col = divmod(device, 16)
    x_lo, z = divmod(row, 4)
    x_hi, rest = divmod(col, 8)
    y, core = divmod(rest, 2)
    return [x_hi * 2 + x_lo, y, z, core]


def device_at(x, y, z, core):
    return ((x % 2) * 4 + z) * 16 + (x // 2) * 8 + y * 2 + core


def shifted(values, axes, step):
    pairs = []
    for source in range(DEVICES):
        place = coords(source)
        axis = axes[place[3]]
        place[axis] = (place[axis] + step) % (2 if axis == 3 else 4)
        pairs.append((source, device_at(*place)))
    return lax.ppermute(values, AXES, pairs)


def ring(block, axes):
    return jnp.concatenate(
        [block, shifted(block, axes, 1), shifted(block, axes, 2), shifted(block, axes, -1)], 0
    )


def merge_kernel(scalar_ref, *refs):
    to = lax.broadcasted_iota(jnp.int32, (192, 192), 0)
    of = lax.broadcasted_iota(jnp.int32, (192, 192), 1)
    head, half, y, core, row = to // 96, (to // 48) % 2, (to // 12) % 4, (to // 6) % 2, to % 6
    behind = (scalar_ref[1] - y) & 3
    source = (behind * 2 + (core ^ scalar_ref[3])) * 24 + half * 12 + row * 2 + head
    order = jnp.where(of == source, 1.0, 0.0).astype(BF16)
    slots = jnp.concatenate([ref[...] for ref in refs[:4]], axis=0)
    ordered = dot(order, slots).astype(BF16)
    for part in range(4):
        lanes = slice(part % 2 * 384, (part % 2 + 1) * 384)
        refs[4][0, part // 2, :, lanes] = ordered[part * 48 : (part + 1) * 48]


def merge(scalars, slots):
    vmem = pl.BlockSpec(memory_space=pltpu.VMEM)
    return pl.pallas_call(
        merge_kernel,
        in_specs=[pl.BlockSpec(memory_space=pltpu.SMEM)] + [vmem] * 4,
        out_shape=jax.ShapeDtypeStruct((1, 2, 48, TOKENS), BF16),
        compiler_params=pltpu.CompilerParams(vmem_limit_bytes=8 * MIB),
        cost_estimate=pl.CostEstimate(flops=10**7, bytes_accessed=3 * 10**5, transcendentals=0),
    )(scalars, *slots)


def gather_plane(place, kept, sent, beside, work, crossing=False):
    block = jnp.concatenate([kept, shifted(sent, (3, 3), 1)], axis=0)
    slots = [block] + [shifted(block, (1, 1), step) for step in (1, 2, -1)]
    if crossing:
        *slots, beside = lax.optimization_barrier((*slots, beside))
        beside = cross(beside)
    block = ring(merge(place, slots), (0, 2))
    block, beside = lax.optimization_barrier((block, beside))
    block = ring(block, (2, 0))
    block, done = lax.optimization_barrier((block, work(beside)))
    return [block, shifted(block, (3, 3), 1)], done


def split(values):
    high = values.astype(BF16)
    return high, (values - high.astype(F32)).astype(BF16)


def dot(a, b, dims=NN):
    return lax.dot_general(a, b, dims, preferred_element_type=F32)


def dot_split(a, b_both):
    both = dot(a, b_both)
    return both[:, :HD] + both[:, HD:]


def side_by_side(values):
    return jnp.concatenate(split(values), axis=1)


def stacked(weight):
    high, low = split(weight)
    return jnp.concatenate(
        [jnp.concatenate([high, low], axis=1), jnp.concatenate([high, low * 0], axis=1)], axis=0
    )


def bias_of(w_bias, normed):
    high, low = split(w_bias)
    rows = jnp.concatenate(
        [jnp.concatenate([high, high], axis=1), jnp.concatenate([low, low * 0], axis=1)], axis=0
    )
    both = dot(rows, side_by_side(normed), NT)
    return both[:HEADS] + both[HEADS:]


def standardize(values):
    mean = jnp.full((2 * HD, HD), 1.0 / HD, BF16)
    centred = values - dot(side_by_side(values), mean)
    spread = dot(side_by_side(centred * centred), mean)
    return centred * lax.rsqrt(spread + EPSILON)


def normalize(values, gain, shift):
    return standardize(values) * gain + shift


def encode(values):
    size = jnp.floor(jnp.log(1.0 + CURVE * jnp.abs(values)) * (1 / CODE_STEP) + 0.5)
    return jnp.where(values < 0, -size, size)


def decode(codes):
    size = (jnp.exp(jnp.abs(codes) * CODE_STEP) - 1.0) * (1 / CURVE)
    return jnp.where(codes < 0, -size, size)


def put_bias(bias, rows_ref, step, count):
    for row in range(count):

        @pl.when(step == row)
        def _():
            for part in range(4):
                pair, half = part // 2, part % 2
                at = pair * 24 + half * 12 + row * 2
                lanes = slice(half * 384, (half + 1) * 384)
                rows_ref[at : at + 2, :] = bias[pair * 2 : pair * 2 + 2, lanes]


def hand_over(scalar_ref, rows_ref, kept_ref, sent_ref):
    first, second = rows_ref[:24, :].astype(BF16), rows_ref[24:, :].astype(BF16)
    kept_ref[...] = jnp.where(scalar_ref[3] == 0, first, second)
    sent_ref[...] = jnp.where(scalar_ref[3] == 0, second, first)


def bias_kernel(scalar_ref, x_ref, gain_ref, shift_ref, w_ref, kept_ref, sent_ref, rows_ref):
    step = pl.program_id(0)
    normed = normalize(x_ref[0], gain_ref[0:1, :], shift_ref[0:1, :])
    put_bias(bias_of(w_ref[0], normed), rows_ref, step, ROWS)

    @pl.when(step == ROWS - 1)
    def _():
        hand_over(scalar_ref, rows_ref, kept_ref, sent_ref)


def small(*shape):
    return pl.BlockSpec(shape, lambda i: (0,) * len(shape))


def first_bias(scalars, x, gain, shift, w_bias):
    return pl.pallas_call(
        bias_kernel,
        grid=(ROWS,),
        in_specs=[
            pl.BlockSpec(memory_space=pltpu.SMEM),
            pl.BlockSpec((1, TOKENS, HD), lambda i: (i, 0, 0)),
            small(2, HD),
            small(2, HD),
            small(2, HEADS, HD),
        ],
        out_specs=[small(24, 384)] * 2,
        out_shape=[jax.ShapeDtypeStruct((24, 384), BF16)] * 2,
        scratch_shapes=[pltpu.VMEM((48, 384), F32)],
        compiler_params=pltpu.CompilerParams(
            vmem_limit_bytes=60 * MIB, dimension_semantics=("arbitrary",)
        ),
        cost_estimate=pl.CostEstimate(flops=10**8, bytes_accessed=2 * 10**6, transcendentals=0),
    )(scalars, x, gain, shift, w_bias)


def lane_group():
    return lax.broadcasted_iota(jnp.int32, (1, HD), 1) // HEAD_DIM


def spreader(source_of):
    row = lax.broadcasted_iota(jnp.int32, (2 * HD, HEADS * HD), 0)
    column = lax.broadcasted_iota(jnp.int32, (2 * HD, HEADS * HD), 1)
    head, group, d = column // HD, (column // HEAD_DIM) % 4, column % HEAD_DIM
    part = source_of(head, group)
    hit = (part >= 0) & (row == part * HD + head * HEAD_DIM + d)
    return jnp.where(hit, 1.0, 0.0).astype(BF16)


def prepare_weights(weights, w_ref, spread_ref):
    for at, weight in enumerate(weights):
        w_ref[at] = stacked(weight)
    spread_ref[0] = spreader(lambda head, group: group % 2)
    spread_ref[1] = spreader(lambda head, group: group // 2)


def project_kernel(
    crossed, x_ref, gain_ref, shift_ref, gs_ref, wq_ref, wk_ref, wv_ref, wg_ref, q_ref, k_ref, v_ref, g_ref,
    w_ref, spread_ref, *rest,
):
    step = pl.program_id(0)

    @pl.when(step == 0)
    def _():
        weights = [wq_ref[0] * (HEAD_DIM**-0.5 * LOG2E), wk_ref[0], wv_ref[0], wg_ref[0]]
        prepare_weights(weights, w_ref, spread_ref)

    if crossed:
        for row in range(ROWS):
            rest[0][pl.ds(row, DEVICES, stride=ROWS), :] = x_ref[
                pl.ds(row * ROWS + step, DEVICES, stride=PADDED), :
            ]
        standard = decode(rest[0][...])
    else:
        standard = standardize(x_ref[0])
    own = slice(int(crossed), int(crossed) + 1)
    cells = side_by_side(standard * gain_ref[own, :] + shift_ref[own, :])

    def columns(at):
        return dot_split(cells, w_ref[at])

    for at, ref in enumerate((q_ref, k_ref)):
        parts = side_by_side(columns(at))
        for pair in range(2):
            cut = slice(pair * 2 * HD, (pair + 1) * 2 * HD)
            spread = dot(parts, spread_ref[at, :, cut]).astype(BF16)
            ref[0, 2 * pair] = spread[:, :HD]
            ref[0, 2 * pair + 1] = spread[:, HD:]
    v_ref[0] = side_by_side(columns(2))
    g_ref[0] = jax.nn.sigmoid(columns(3) + gs_ref[own, :])


def matrix(second):
    return pl.BlockSpec((1, HD, HD), lambda i: (int(second), 0, 0))


def project(crossed, x, vectors, matrices):
    whole = pl.BlockSpec(memory_space=pltpu.VMEM)
    row_spec = pl.BlockSpec((1, TOKENS, HD), lambda i: (i, 0, 0))
    head_spec = pl.BlockSpec((1, HEADS, TOKENS, HD), lambda i: (i, 0, 0, 0))
    scratch = [
        pltpu.VMEM((4, 2 * HD, 2 * HD), BF16),
        pltpu.VMEM((2, 2 * HD, HEADS * HD), BF16),
    ]
    if crossed:
        scratch.append(pltpu.VMEM((TOKENS, HD), F32))
    return pl.pallas_call(
        functools.partial(project_kernel, crossed),
        grid=(ROWS,),
        in_specs=[whole if crossed else row_spec] + [small(2, HD)] * 3 + [matrix(crossed)] * 4,
        out_specs=[
            head_spec, head_spec, pl.BlockSpec((1, TOKENS, 2 * HD), lambda i: (i, 0, 0)), row_spec,
        ],
        out_shape=[
            jax.ShapeDtypeStruct((ROWS, HEADS, TOKENS, HD), BF16),
            jax.ShapeDtypeStruct((ROWS, HEADS, TOKENS, HD), BF16),
            jax.ShapeDtypeStruct((ROWS, TOKENS, 2 * HD), BF16),
            jax.ShapeDtypeStruct((ROWS, TOKENS, HD), F32),
        ],
        scratch_shapes=scratch,
        compiler_params=pltpu.CompilerParams(
            vmem_limit_bytes=24 * MIB, dimension_semantics=("arbitrary",)
        ),
        cost_estimate=pl.CostEstimate(
            flops=10**10, bytes_accessed=17 * 10**6, transcendentals=10**6
        ),
    )(x, *vectors, *matrices)


def build_plane(scalar_ref, piece_refs, plane_ref, flat_ref, turned):
    my_x, my_z, core, real = scalar_ref[0], scalar_ref[2], scalar_ref[3], scalar_ref[4]
    limit = ((real + 255) // 256) * 256

    def one_group(group, _):
        x_hi, z, x_lo = group % 2, (group // 2) % 4, group // 8
        behind_x, behind_z = (my_x - (x_hi * 2 + x_lo)) & 3, (my_z - z) & 3
        rows = pl.ds(pl.multiple_of(group * 48, 16), 48)
        for ref, pair in zip(piece_refs, (core, 1 - core)):
            at = jnp.where(pair == 0, behind_z * 4 + behind_x, behind_x * 4 + behind_z)
            for half in range(2):
                lanes = slice(half * 384, (half + 1) * 384)

                @pl.when(group * 48 < limit if turned else half * 384 < limit)
                def _():
                    for odd in range(2):
                        values = ref[at, odd, :, lanes]
                        if turned:
                            flat_ref[pair * 2 + odd, rows, lanes] = values
                        else:
                            key = lax.broadcasted_iota(jnp.int32, (48, 384), 1) + half * 384
                            plane_ref[pair * 2 + odd, rows, lanes] = jnp.where(
                                key < real, values.astype(F32) * LOG2E, NEGATIVE
                            )
        return 0

    lax.fori_loop(0, 16, one_group, 0)

    def turn(head, _):
        for block in range(6):
            keys = slice(block * 128, block * 128 + 128)

            @pl.when(block * 128 < limit)
            def _():
                live = lax.broadcasted_iota(jnp.int32, (128, 128), 1) + block * 128 < real
                for other in range(6):
                    rows = slice(other * 128, other * 128 + 128)
                    values = flat_ref[head, keys, rows].T.astype(F32) * LOG2E
                    plane_ref[head, rows, keys] = jnp.where(live, values, NEGATIVE)
        return 0

    if turned:
        lax.fori_loop(0, HEADS, turn, 0)


def attend(keys, q_ref, k_ref, v_ref, plane_ref):
    group = lane_group()
    value = total = None
    for head in range(HEADS):
        scores = dot(q_ref[0, head], k_ref[0, head, :keys, :], NT) + plane_ref[head, :, :keys]
        highest = jnp.max(scores, axis=-1, keepdims=True)
        weights = jnp.exp2(scores - highest).astype(BF16)
        weight = jnp.sum(weights.astype(F32), axis=-1, keepdims=True)
        mixed = dot(weights, v_ref[0, :keys, :])
        mixed = mixed[:, :HD] + mixed[:, HD:]
        weight = jnp.broadcast_to(weight, mixed.shape)
        value = mixed if head == 0 else jnp.where(group == head, mixed, value)
        total = weight if head == 0 else jnp.where(group == head, weight, total)
    return value / total


def attend_kernel(turned, scalar_ref, q_ref, k_ref, v_ref, g_ref, wo_ref, *rest):
    piece_refs, rest = rest[:2], rest[2:]
    step = pl.program_id(0)
    before = jnp.maximum(step - 1, 0)
    if turned:
        crossed_ref, plane_ref, mixed_ref, gated_ref, flat_ref = rest
    else:
        x_ref, gain_ref, shift_ref, nbias_ref = rest[:4]
        first_ref, crossed_ref, kept_ref, sent_ref = rest[4:8]
        plane_ref, mixed_ref, gated_ref, rows_ref, wide_ref, bias_ref = rest[8:]

    @pl.when(step == 0)
    def _():
        gated_ref[...] = jnp.zeros_like(gated_ref)
        build_plane(scalar_ref, piece_refs, plane_ref, flat_ref if turned else None, turned)
        if not turned:
            wide_ref[...] = jnp.zeros_like(wide_ref)

    def finish():
        update = dot_split(gated_ref[...], stacked(wo_ref[0]))
        if turned:
            mixed_ref[...] = update
            for row in range(ROWS):
                crossed_ref[pl.ds(row * ROWS + before, DEVICES, stride=PADDED), :] = mixed_ref[
                    pl.ds(row, DEVICES, stride=ROWS), :
                ]
        else:
            first = x_ref[0] + update
            first_ref[0] = first
            standard = standardize(first)
            mixed_ref[...] = encode(standard)
            for column in range(ROWS):
                wide_ref[pl.ds(before * ROWS + column, DEVICES, stride=PADDED), :] = mixed_ref[
                    pl.ds(column, DEVICES, stride=ROWS), :
                ]
            normed = standard * gain_ref[1:2, :] + shift_ref[1:2, :]
            bias_ref[:HEADS, :] = bias_of(nbias_ref[1], normed)

    real = scalar_ref[4]
    for keys in (256, 512, 768):

        @pl.when((step < ROWS) & (real > keys - 256) & (real <= keys))
        def _():
            finish()
            mixed = attend(keys, q_ref, k_ref, v_ref, plane_ref)
            gated_ref[...] = side_by_side(g_ref[0] * mixed)

    @pl.when(step == ROWS)
    def _():
        finish()

    if not turned:
        put_bias(bias_ref[:HEADS, :], rows_ref, step - 1, ROWS)

        @pl.when(step == ROWS)
        def _():
            crossed_ref[...] = wide_ref[...].astype(jnp.int32).astype(jnp.int16)
            hand_over(scalar_ref, rows_ref, kept_ref, sent_ref)


def run_pass(turned, scalars, projected, w_o, pieces, x=None, extra=()):
    whole = pl.BlockSpec(memory_space=pltpu.VMEM)
    now, last = (lambda i: jnp.minimum(i, ROWS - 1)), (lambda i: jnp.maximum(i - 1, 0))
    row_spec = pl.BlockSpec((1, TOKENS, HD), lambda i: (now(i), 0, 0))
    last_spec = pl.BlockSpec((1, TOKENS, HD), lambda i: (last(i), 0, 0))
    head_spec = pl.BlockSpec((1, HEADS, TOKENS, HD), lambda i: (now(i), 0, 0, 0))
    in_specs = [pl.BlockSpec(memory_space=pltpu.SMEM), head_spec, head_spec]
    in_specs += [pl.BlockSpec((1, TOKENS, 2 * HD), lambda i: (now(i), 0, 0)), row_spec]
    in_specs += [matrix(turned)] + [whole] * 2
    out_shape = [jax.ShapeDtypeStruct((DEVICES * PADDED, HD), F32 if turned else jnp.int16)]
    out_specs = [pl.BlockSpec((DEVICES * PADDED, HD), lambda i: (0, 0))]
    scratch = [pltpu.VMEM((HEADS, TOKENS, TOKENS), F32), pltpu.VMEM((TOKENS, HD), F32)]
    scratch.append(pltpu.VMEM((TOKENS, 2 * HD), BF16))
    if turned:
        scratch.append(pltpu.VMEM((HEADS, TOKENS, TOKENS), BF16))
    args = [scalars, *projected, w_o, *pieces]
    if not turned:
        in_specs += [last_spec, small(2, HD), small(2, HD), small(2, HEADS, HD)]
        args += [x, *extra]
        out_shape = [jax.ShapeDtypeStruct((ROWS, TOKENS, HD), F32)] + out_shape
        out_shape += [jax.ShapeDtypeStruct((24, 384), BF16)] * 2
        out_specs = [last_spec] + out_specs + [pl.BlockSpec((24, 384), lambda i: (0, 0))] * 2
        scratch += [pltpu.VMEM((48, 384), F32), pltpu.VMEM((DEVICES * PADDED, HD), F32)]
        scratch.append(pltpu.VMEM((8, TOKENS), F32))
    return pl.pallas_call(
        functools.partial(attend_kernel, turned),
        grid=(ROWS + 1,),
        in_specs=in_specs,
        out_specs=out_specs,
        out_shape=out_shape,
        scratch_shapes=scratch,
        compiler_params=pltpu.CompilerParams(
            vmem_limit_bytes=26 * MIB, dimension_semantics=("arbitrary",)
        ),
        cost_estimate=pl.CostEstimate(
            flops=2 * 10**10, bytes_accessed=2 * 10**7, transcendentals=14 * 10**6
        ),
    )(*args)


def final_kernel(first_ref, update_ref, out_ref, row_ref):
    step = pl.program_id(0)
    for column in range(ROWS):
        row_ref[pl.ds(column, DEVICES, stride=ROWS), :] = update_ref[
            pl.ds(step * ROWS + column, DEVICES, stride=PADDED), :
        ]
    out_ref[0] = first_ref[0] + row_ref[...]


def add_crossed(first, update):
    row_spec = pl.BlockSpec((1, TOKENS, HD), lambda i: (i, 0, 0))
    return pl.pallas_call(
        final_kernel,
        grid=(ROWS,),
        in_specs=[row_spec, pl.BlockSpec(memory_space=pltpu.VMEM)],
        out_specs=row_spec,
        out_shape=jax.ShapeDtypeStruct((ROWS, TOKENS, HD), F32),
        scratch_shapes=[pltpu.VMEM((TOKENS, HD), F32)],
        compiler_params=pltpu.CompilerParams(
            vmem_limit_bytes=16 * MIB, dimension_semantics=("arbitrary",)
        ),
        cost_estimate=pl.CostEstimate(flops=10**6, bytes_accessed=8 * 10**6, transcendentals=0),
    )(first, update)


def cross(values):
    return lax.all_to_all(values, AXES, split_axis=0, concat_axis=0, tiled=True)


def on_device(
    pair_tensor,
    token_mask,
    ln_gain,
    ln_shift,
    w_query,
    w_key,
    w_value,
    w_bias,
    w_gate,
    gate_shift,
    w_out,
):
    row, col = lax.axis_index("row"), lax.axis_index("col")
    place = [(col // 8) * 2 + row // 4, (col // 2) % 4, row % 4, col % 2]
    place = jnp.stack([jnp.int32(p) for p in place])
    vectors, matrices = (ln_gain, ln_shift, gate_shift), (w_query, w_key, w_value, w_gate)

    start = first_bias(place, pair_tensor, ln_gain, ln_shift, w_bias)
    scalars = jnp.concatenate([place, jnp.sum(token_mask, dtype=jnp.int32, keepdims=True)])
    planes, (projected, scalars) = gather_plane(
        place, *start, (pair_tensor, scalars),
        lambda held: (project(False, held[0], vectors, matrices), held[1]),
    )
    first, codes, *end = run_pass(
        False, scalars, projected, w_out, planes, pair_tensor, (ln_gain, ln_shift, w_bias)
    )
    planes, projected = gather_plane(
        place, *end, codes, lambda held: project(True, held.astype(F32), vectors, matrices), True
    )
    (update,) = run_pass(True, scalars, projected, w_out, planes)
    return add_crossed(first, cross(update.astype(jnp.float16)).astype(F32))


def solution(mesh):
    placed = (P(AXES, None, None), P(), P(), P(), P(), P(), P(), P(), P(), P(), P())
    return jax.shard_map(
        on_device,
        mesh=mesh,
        in_specs=placed,
        out_specs=P(AXES, None, None),
        check_vma=False,
    )
```

```python
import functools

import jax
import jax.numpy as jnp
import numpy as np
from jax import lax
from jax.experimental import pallas as pl
from jax.experimental.pallas import tpu as pltpu
from jax.sharding import PartitionSpec as P

HEADS = 4
HEAD_DIM = 32
HD = 128
TOKENS = 768
ROWS = 6
DEVICES = 128
PADDED = 40
EPSILON = 1e-05
NEGATIVE = -1e30
LOG2E = 1.4426950408889634
CURVE = 4.0
CODE_STEP = float(np.log(1 + CURVE * 11.32) / 32767)
AXES = ("row", "col")
MIB = 1024 * 1024
F32, BF16 = jnp.float32, jnp.bfloat16
NT = (((1,), (1,)), ((), ()))
NN = (((1,), (0,)), ((), ()))


def coords(device):
    row, col = divmod(device, 16)
    x_lo, z = divmod(row, 4)
    x_hi, rest = divmod(col, 8)
    y, core = divmod(rest, 2)
    return [x_hi * 2 + x_lo, y, z, core]


def device_at(x, y, z, core):
    return ((x % 2) * 4 + z) * 16 + (x // 2) * 8 + y * 2 + core


def shifted(values, axes, step):
    pairs = []
    for source in range(DEVICES):
        place = coords(source)
        axis = axes[place[3]]
        place[axis] = (place[axis] + step) % (2 if axis == 3 else 4)
        pairs.append((source, device_at(*place)))
    return lax.ppermute(values, AXES, pairs)


def ring(block, axes):
    return [block] + [shifted(block, axes, step) for step in (1, 2, -1)]


def merge_kernel(scalar_ref, *refs):
    to = lax.broadcasted_iota(jnp.int32, (192, 192), 0)
    of = lax.broadcasted_iota(jnp.int32, (192, 192), 1)
    head, half, y, core, row = to // 96, (to // 48) % 2, (to // 12) % 4, (to // 6) % 2, to % 6
    behind = (scalar_ref[1] - y) & 3
    source = (behind * 2 + (core ^ scalar_ref[3])) * 24 + half * 12 + row * 2 + head
    order = jnp.where(of == source, 1.0, 0.0).astype(BF16)
    slots = jnp.concatenate([ref[...] for ref in refs[:4]], axis=0)
    ordered = dot(order, slots).astype(BF16)
    for part in range(4):
        lanes = slice(part % 2 * 384, (part % 2 + 1) * 384)
        refs[4][0, part // 2, :, lanes] = ordered[part * 48 : (part + 1) * 48]


def merge(scalars, slots):
    vmem = pl.BlockSpec(memory_space=pltpu.VMEM)
    return pl.pallas_call(
        merge_kernel,
        in_specs=[pl.BlockSpec(memory_space=pltpu.SMEM)] + [vmem] * 4,
        out_shape=jax.ShapeDtypeStruct((1, 2, 48, TOKENS), BF16),
        compiler_params=pltpu.CompilerParams(vmem_limit_bytes=8 * MIB),
        cost_estimate=pl.CostEstimate(flops=10**7, bytes_accessed=3 * 10**5, transcendentals=0),
    )(scalars, *slots)


def gather_plane(place, kept, sent, beside, work, crossing=False):
    block = jnp.concatenate([kept, shifted(sent, (3, 3), 1)], axis=0)
    slots = [block] + [shifted(block, (1, 1), step) for step in (1, 2, -1)]
    if crossing:
        *slots, beside = lax.optimization_barrier((*slots, beside))
        beside = cross(beside)
    block = jnp.concatenate(ring(merge(place, slots), (0, 2)), axis=0)
    block, beside = lax.optimization_barrier((block, beside))
    blocks = ring(block, (2, 0))
    done = work(beside)
    others = [shifted(block, (3, 3), 1)]
    for at in (3, 1, 2):
        blocks[at], done = lax.optimization_barrier((blocks[at], done))
    others += [shifted(blocks[at], (3, 3), 1) for at in (1, 2, 3)]
    return blocks + others, done


def split(values):
    high = values.astype(BF16)
    return high, (values - high.astype(F32)).astype(BF16)


def dot(a, b, dims=NN):
    return lax.dot_general(a, b, dims, preferred_element_type=F32)


def dot_split(a, b_both):
    both = dot(a, b_both)
    return both[:, :HD] + both[:, HD:]


def side_by_side(values):
    return jnp.concatenate(split(values), axis=1)


def stacked(weight):
    high, low = split(weight)
    return jnp.concatenate(
        [jnp.concatenate([high, low], axis=1), jnp.concatenate([high, low * 0], axis=1)], axis=0
    )


def bias_of(w_bias, normed):
    high, low = split(w_bias)
    rows = jnp.concatenate(
        [jnp.concatenate([high, high], axis=1), jnp.concatenate([low, low * 0], axis=1)], axis=0
    )
    both = dot(rows, side_by_side(normed), NT)
    return both[:HEADS] + both[HEADS:]


def standardize(values):
    mean = jnp.full((2 * HD, HD), 1.0 / HD, BF16)
    centred = values - dot(side_by_side(values), mean)
    spread = dot(side_by_side(centred * centred), mean)
    return centred * lax.rsqrt(spread + EPSILON)


def normalize(values, gain, shift):
    return standardize(values) * gain + shift


def encode(values):
    size = jnp.floor(jnp.log(1.0 + CURVE * jnp.abs(values)) * (1 / CODE_STEP) + 0.5)
    return jnp.where(values < 0, -size, size)


def decode(codes):
    size = (jnp.exp(jnp.abs(codes) * CODE_STEP) - 1.0) * (1 / CURVE)
    return jnp.where(codes < 0, -size, size)


def put_bias(bias, rows_ref, step, count):
    for row in range(count):

        @pl.when(step == row)
        def _():
            for part in range(4):
                pair, half = part // 2, part % 2
                at = pair * 24 + half * 12 + row * 2
                lanes = slice(half * 384, (half + 1) * 384)
                rows_ref[at : at + 2, :] = bias[pair * 2 : pair * 2 + 2, lanes]


def hand_over(scalar_ref, rows_ref, kept_ref, sent_ref):
    first, second = rows_ref[:24, :].astype(BF16), rows_ref[24:, :].astype(BF16)
    kept_ref[...] = jnp.where(scalar_ref[3] == 0, first, second)
    sent_ref[...] = jnp.where(scalar_ref[3] == 0, second, first)


def bias_kernel(scalar_ref, x_ref, gain_ref, shift_ref, w_ref, kept_ref, sent_ref, rows_ref):
    step = pl.program_id(0)
    normed = normalize(x_ref[0], gain_ref[0:1, :], shift_ref[0:1, :])
    put_bias(bias_of(w_ref[0], normed), rows_ref, step, ROWS)

    @pl.when(step == ROWS - 1)
    def _():
        hand_over(scalar_ref, rows_ref, kept_ref, sent_ref)


def small(*shape):
    return pl.BlockSpec(shape, lambda i: (0,) * len(shape))


def first_bias(scalars, x, gain, shift, w_bias):
    return pl.pallas_call(
        bias_kernel,
        grid=(ROWS,),
        in_specs=[
            pl.BlockSpec(memory_space=pltpu.SMEM),
            pl.BlockSpec((1, TOKENS, HD), lambda i: (i, 0, 0)),
            small(2, HD),
            small(2, HD),
            small(2, HEADS, HD),
        ],
        out_specs=[small(24, 384)] * 2,
        out_shape=[jax.ShapeDtypeStruct((24, 384), BF16)] * 2,
        scratch_shapes=[pltpu.VMEM((48, 384), F32)],
        compiler_params=pltpu.CompilerParams(
            vmem_limit_bytes=60 * MIB, dimension_semantics=("arbitrary",)
        ),
        cost_estimate=pl.CostEstimate(flops=10**8, bytes_accessed=2 * 10**6, transcendentals=0),
    )(scalars, x, gain, shift, w_bias)


def lane_group():
    return lax.broadcasted_iota(jnp.int32, (1, HD), 1) // HEAD_DIM


def spreader(source_of):
    row = lax.broadcasted_iota(jnp.int32, (2 * HD, HEADS * HD), 0)
    column = lax.broadcasted_iota(jnp.int32, (2 * HD, HEADS * HD), 1)
    head, group, d = column // HD, (column // HEAD_DIM) % 4, column % HEAD_DIM
    part = source_of(head, group)
    hit = (part >= 0) & (row == part * HD + head * HEAD_DIM + d)
    return jnp.where(hit, 1.0, 0.0).astype(BF16)


def prepare_weights(weights, w_ref, spread_ref):
    for at, weight in enumerate(weights):
        w_ref[at] = stacked(weight)
    spread_ref[0] = spreader(lambda head, group: group % 2)
    spread_ref[1] = spreader(lambda head, group: group // 2)


def project_kernel(
    crossed, x_ref, gain_ref, shift_ref, gs_ref, wq_ref, wk_ref, wv_ref, wg_ref, q_ref, k_ref, v_ref, g_ref,
    w_ref, spread_ref, *rest,
):
    step = pl.program_id(0)

    @pl.when(step == 0)
    def _():
        weights = [wq_ref[0] * (HEAD_DIM**-0.5 * LOG2E), wk_ref[0], wv_ref[0], wg_ref[0]]
        prepare_weights(weights, w_ref, spread_ref)

    if crossed:
        for row in range(ROWS):
            rest[0][pl.ds(row, DEVICES, stride=ROWS), :] = x_ref[
                pl.ds(row * ROWS + step, DEVICES, stride=PADDED), :
            ]
        standard = decode(rest[0][...])
    else:
        standard = standardize(x_ref[0])
    own = slice(int(crossed), int(crossed) + 1)
    cells = side_by_side(standard * gain_ref[own, :] + shift_ref[own, :])

    def columns(at):
        return dot_split(cells, w_ref[at])

    for at, ref in enumerate((q_ref, k_ref)):
        parts = side_by_side(columns(at))
        for pair in range(2):
            cut = slice(pair * 2 * HD, (pair + 1) * 2 * HD)
            spread = dot(parts, spread_ref[at, :, cut]).astype(BF16)
            ref[0, 2 * pair] = spread[:, :HD]
            ref[0, 2 * pair + 1] = spread[:, HD:]
    v_ref[0] = side_by_side(columns(2))
    g_ref[0] = jax.nn.sigmoid(columns(3) + gs_ref[own, :])


def matrix(second):
    return pl.BlockSpec((1, HD, HD), lambda i: (int(second), 0, 0))


def project(crossed, x, vectors, matrices):
    whole = pl.BlockSpec(memory_space=pltpu.VMEM)
    row_spec = pl.BlockSpec((1, TOKENS, HD), lambda i: (i, 0, 0))
    head_spec = pl.BlockSpec((1, HEADS, TOKENS, HD), lambda i: (i, 0, 0, 0))
    scratch = [
        pltpu.VMEM((4, 2 * HD, 2 * HD), BF16),
        pltpu.VMEM((2, 2 * HD, HEADS * HD), BF16),
    ]
    if crossed:
        scratch.append(pltpu.VMEM((TOKENS, HD), F32))
    return pl.pallas_call(
        functools.partial(project_kernel, crossed),
        grid=(ROWS,),
        in_specs=[whole if crossed else row_spec] + [small(2, HD)] * 3 + [matrix(crossed)] * 4,
        out_specs=[
            head_spec, head_spec, pl.BlockSpec((1, TOKENS, 2 * HD), lambda i: (i, 0, 0)), row_spec,
        ],
        out_shape=[
            jax.ShapeDtypeStruct((ROWS, HEADS, TOKENS, HD), BF16),
            jax.ShapeDtypeStruct((ROWS, HEADS, TOKENS, HD), BF16),
            jax.ShapeDtypeStruct((ROWS, TOKENS, 2 * HD), BF16),
            jax.ShapeDtypeStruct((ROWS, TOKENS, HD), F32),
        ],
        scratch_shapes=scratch,
        compiler_params=pltpu.CompilerParams(
            vmem_limit_bytes=24 * MIB, dimension_semantics=("arbitrary",)
        ),
        cost_estimate=pl.CostEstimate(
            flops=10**10, bytes_accessed=17 * 10**6, transcendentals=10**6
        ),
    )(x, *vectors, *matrices)


def build_plane(scalar_ref, piece_refs, plane_ref, flat_ref, turned):
    my_x, my_z, core, real = scalar_ref[0], scalar_ref[2], scalar_ref[3], scalar_ref[4]
    limit = ((real + 255) // 256) * 256

    def one_slot(inner, _):
        for ref, outer, pair in zip(piece_refs, (0, 1, 2, 3) * 2, (core,) * 4 + (1 - core,) * 4):
            x = (my_x - jnp.where(pair == 0, inner, outer)) & 3
            z = (my_z - jnp.where(pair == 0, outer, inner)) & 3
            group = (x & 1) * 8 + z * 2 + x // 2
            rows = pl.ds(pl.multiple_of(group * 48, 16), 48)
            for half in range(2):
                lanes = slice(half * 384, (half + 1) * 384)

                @pl.when(group * 48 < limit if turned else half * 384 < limit)
                def _():
                    for odd in range(2):
                        values = ref[inner, odd, :, lanes]
                        if turned:
                            flat_ref[pair * 2 + odd, rows, lanes] = values
                        else:
                            key = lax.broadcasted_iota(jnp.int32, (48, 384), 1) + half * 384
                            plane_ref[pair * 2 + odd, rows, lanes] = jnp.where(
                                key < real, values.astype(F32) * LOG2E, NEGATIVE
                            )
        return 0

    lax.fori_loop(0, 4, one_slot, 0)

    def turn(head, _):
        for block in range(6):
            keys = slice(block * 128, block * 128 + 128)

            @pl.when(block * 128 < limit)
            def _():
                live = lax.broadcasted_iota(jnp.int32, (128, 128), 1) + block * 128 < real
                for other in range(6):
                    rows = slice(other * 128, other * 128 + 128)
                    values = flat_ref[head, keys, rows].T.astype(F32) * LOG2E
                    plane_ref[head, rows, keys] = jnp.where(live, values, NEGATIVE)
        return 0

    if turned:
        lax.fori_loop(0, HEADS, turn, 0)


def attend(keys, q_ref, k_ref, v_ref, plane_ref):
    group = lane_group()
    value = total = None
    for head in range(HEADS):
        scores = dot(q_ref[0, head], k_ref[0, head, :keys, :], NT) + plane_ref[head, :, :keys]
        highest = jnp.max(scores, axis=-1, keepdims=True)
        weights = jnp.exp2(scores - highest).astype(BF16)
        weight = jnp.sum(weights.astype(F32), axis=-1, keepdims=True)
        mixed = dot(weights, v_ref[0, :keys, :])
        mixed = mixed[:, :HD] + mixed[:, HD:]
        weight = jnp.broadcast_to(weight, mixed.shape)
        value = mixed if head == 0 else jnp.where(group == head, mixed, value)
        total = weight if head == 0 else jnp.where(group == head, weight, total)
    return value / total


def attend_kernel(turned, scalar_ref, q_ref, k_ref, v_ref, g_ref, wo_ref, *rest):
    piece_refs, rest = rest[:8], rest[8:]
    step = pl.program_id(0)
    before = jnp.maximum(step - 1, 0)
    if turned:
        crossed_ref, plane_ref, mixed_ref, gated_ref, flat_ref = rest
    else:
        x_ref, gain_ref, shift_ref, nbias_ref = rest[:4]
        first_ref, crossed_ref, kept_ref, sent_ref = rest[4:8]
        plane_ref, mixed_ref, gated_ref, rows_ref, wide_ref, bias_ref = rest[8:]

    @pl.when(step == 0)
    def _():
        gated_ref[...] = jnp.zeros_like(gated_ref)
        build_plane(scalar_ref, piece_refs, plane_ref, flat_ref if turned else None, turned)
        if not turned:
            wide_ref[...] = jnp.zeros_like(wide_ref)

    def finish():
        update = dot_split(gated_ref[...], stacked(wo_ref[0]))
        if turned:
            mixed_ref[...] = update
            for row in range(ROWS):
                crossed_ref[pl.ds(row * ROWS + before, DEVICES, stride=PADDED), :] = mixed_ref[
                    pl.ds(row, DEVICES, stride=ROWS), :
                ]
        else:
            first = x_ref[0] + update
            first_ref[0] = first
            standard = standardize(first)
            mixed_ref[...] = encode(standard)
            for column in range(ROWS):
                wide_ref[pl.ds(before * ROWS + column, DEVICES, stride=PADDED), :] = mixed_ref[
                    pl.ds(column, DEVICES, stride=ROWS), :
                ]
            normed = standard * gain_ref[1:2, :] + shift_ref[1:2, :]
            bias_ref[:HEADS, :] = bias_of(nbias_ref[1], normed)

    real = scalar_ref[4]
    for keys in (256, 512, 768):

        @pl.when((step < ROWS) & (real > keys - 256) & (real <= keys))
        def _():
            finish()
            mixed = attend(keys, q_ref, k_ref, v_ref, plane_ref)
            gated_ref[...] = side_by_side(g_ref[0] * mixed)

    @pl.when(step == ROWS)
    def _():
        finish()

    if not turned:
        put_bias(bias_ref[:HEADS, :], rows_ref, step - 1, ROWS)

        @pl.when(step == ROWS)
        def _():
            crossed_ref[...] = wide_ref[...].astype(jnp.int32).astype(jnp.int16)
            hand_over(scalar_ref, rows_ref, kept_ref, sent_ref)


def run_pass(turned, scalars, projected, w_o, pieces, x=None, extra=()):
    whole = pl.BlockSpec(memory_space=pltpu.VMEM)
    now, last = (lambda i: jnp.minimum(i, ROWS - 1)), (lambda i: jnp.maximum(i - 1, 0))
    row_spec = pl.BlockSpec((1, TOKENS, HD), lambda i: (now(i), 0, 0))
    last_spec = pl.BlockSpec((1, TOKENS, HD), lambda i: (last(i), 0, 0))
    head_spec = pl.BlockSpec((1, HEADS, TOKENS, HD), lambda i: (now(i), 0, 0, 0))
    in_specs = [pl.BlockSpec(memory_space=pltpu.SMEM), head_spec, head_spec]
    in_specs += [pl.BlockSpec((1, TOKENS, 2 * HD), lambda i: (now(i), 0, 0)), row_spec]
    in_specs += [matrix(turned)] + [whole] * 8
    out_shape = [jax.ShapeDtypeStruct((DEVICES * PADDED, HD), F32 if turned else jnp.int16)]
    out_specs = [pl.BlockSpec((DEVICES * PADDED, HD), lambda i: (0, 0))]
    scratch = [pltpu.VMEM((HEADS, TOKENS, TOKENS), F32), pltpu.VMEM((TOKENS, HD), F32)]
    scratch.append(pltpu.VMEM((TOKENS, 2 * HD), BF16))
    if turned:
        scratch.append(pltpu.VMEM((HEADS, TOKENS, TOKENS), BF16))
    args = [scalars, *projected, w_o, *pieces]
    if not turned:
        in_specs += [last_spec, small(2, HD), small(2, HD), small(2, HEADS, HD)]
        args += [x, *extra]
        out_shape = [jax.ShapeDtypeStruct((ROWS, TOKENS, HD), F32)] + out_shape
        out_shape += [jax.ShapeDtypeStruct((24, 384), BF16)] * 2
        out_specs = [last_spec] + out_specs + [pl.BlockSpec((24, 384), lambda i: (0, 0))] * 2
        scratch += [pltpu.VMEM((48, 384), F32), pltpu.VMEM((DEVICES * PADDED, HD), F32)]
        scratch.append(pltpu.VMEM((8, TOKENS), F32))
    return pl.pallas_call(
        functools.partial(attend_kernel, turned),
        grid=(ROWS + 1,),
        in_specs=in_specs,
        out_specs=out_specs,
        out_shape=out_shape,
        scratch_shapes=scratch,
        compiler_params=pltpu.CompilerParams(
            vmem_limit_bytes=26 * MIB, dimension_semantics=("arbitrary",)
        ),
        cost_estimate=pl.CostEstimate(
            flops=2 * 10**10, bytes_accessed=2 * 10**7, transcendentals=14 * 10**6
        ),
    )(*args)


def final_kernel(first_ref, update_ref, out_ref, row_ref):
    step = pl.program_id(0)
    for column in range(ROWS):
        row_ref[pl.ds(column, DEVICES, stride=ROWS), :] = update_ref[
            pl.ds(step * ROWS + column, DEVICES, stride=PADDED), :
        ]
    out_ref[0] = first_ref[0] + row_ref[...]


def add_crossed(first, update):
    row_spec = pl.BlockSpec((1, TOKENS, HD), lambda i: (i, 0, 0))
    return pl.pallas_call(
        final_kernel,
        grid=(ROWS,),
        in_specs=[row_spec, pl.BlockSpec(memory_space=pltpu.VMEM)],
        out_specs=row_spec,
        out_shape=jax.ShapeDtypeStruct((ROWS, TOKENS, HD), F32),
        scratch_shapes=[pltpu.VMEM((TOKENS, HD), F32)],
        compiler_params=pltpu.CompilerParams(
            vmem_limit_bytes=16 * MIB, dimension_semantics=("arbitrary",)
        ),
        cost_estimate=pl.CostEstimate(flops=10**6, bytes_accessed=8 * 10**6, transcendentals=0),
    )(first, update)


def cross(values):
    return lax.all_to_all(values, AXES, split_axis=0, concat_axis=0, tiled=True)


def on_device(
    pair_tensor,
    token_mask,
    ln_gain,
    ln_shift,
    w_query,
    w_key,
    w_value,
    w_bias,
    w_gate,
    gate_shift,
    w_out,
):
    row, col = lax.axis_index("row"), lax.axis_index("col")
    place = [(col // 8) * 2 + row // 4, (col // 2) % 4, row % 4, col % 2]
    place = jnp.stack([jnp.int32(p) for p in place])
    vectors, matrices = (ln_gain, ln_shift, gate_shift), (w_query, w_key, w_value, w_gate)

    start = first_bias(place, pair_tensor, ln_gain, ln_shift, w_bias)
    scalars = jnp.concatenate([place, jnp.sum(token_mask, dtype=jnp.int32, keepdims=True)])
    planes, (projected, scalars) = gather_plane(
        place, *start, (pair_tensor, scalars),
        lambda held: (project(False, held[0], vectors, matrices), held[1]),
    )
    first, codes, *end = run_pass(
        False, scalars, projected, w_out, planes, pair_tensor, (ln_gain, ln_shift, w_bias)
    )
    planes, projected = gather_plane(
        place, *end, codes, lambda held: project(True, held.astype(F32), vectors, matrices), True
    )
    (update,) = run_pass(True, scalars, projected, w_out, planes)
    return add_crossed(first, cross(update.astype(jnp.float16)).astype(F32))


def solution(mesh):
    placed = (P(AXES, None, None), P(), P(), P(), P(), P(), P(), P(), P(), P(), P())
    return jax.shard_map(
        on_device,
        mesh=mesh,
        in_specs=placed,
        out_specs=P(AXES, None, None),
        check_vma=False,
    )
```

```python
import functools

import jax
import jax.numpy as jnp
import numpy as np
from jax import lax
from jax.experimental import pallas as pl
from jax.experimental.pallas import tpu as pltpu
from jax.sharding import PartitionSpec as P

HEADS = 4
HEAD_DIM = 32
HD = 128
TOKENS = 768
ROWS = 6
DEVICES = 128
PADDED = 40
EPSILON = 1e-05
BIAS_ROWS = 3
NEGATIVE = -1e30
LOG2E = 1.4426950408889634
CURVE = 4.0
CODE_STEP = float(np.log(1 + CURVE * 11.32) / 32767)
AXES = ("row", "col")
MIB = 1024 * 1024
F32, BF16 = jnp.float32, jnp.bfloat16
NT = (((1,), (1,)), ((), ()))
NN = (((1,), (0,)), ((), ()))


def coords(device):
    row, col = divmod(device, 16)
    x_lo, z = divmod(row, 4)
    x_hi, rest = divmod(col, 8)
    y, core = divmod(rest, 2)
    return [x_hi * 2 + x_lo, y, z, core]


def device_at(x, y, z, core):
    return ((x % 2) * 4 + z) * 16 + (x // 2) * 8 + y * 2 + core


def shifted(values, axes, step):
    pairs = []
    for source in range(DEVICES):
        place = coords(source)
        axis = axes[place[3]]
        place[axis] = (place[axis] + step) % (2 if axis == 3 else 4)
        pairs.append((source, device_at(*place)))
    return lax.ppermute(values, AXES, pairs)


def ring(block, axes):
    return [block] + [shifted(block, axes, step) for step in (1, 2, -1)]


def merge_kernel(scalar_ref, *refs):
    to = lax.broadcasted_iota(jnp.int32, (192, 192), 0)
    of = lax.broadcasted_iota(jnp.int32, (192, 192), 1)
    head, half, y, core, row = to // 96, (to // 48) % 2, (to // 12) % 4, (to // 6) % 2, to % 6
    behind = (scalar_ref[1] - y) & 3
    source = (behind * 2 + (core ^ scalar_ref[3])) * 24 + half * 12 + row * 2 + head
    order = jnp.where(of == source, 1.0, 0.0).astype(BF16)
    slots = jnp.concatenate([ref[...] for ref in refs[:4]], axis=0)
    ordered = dot(order, slots).astype(BF16)
    for part in range(4):
        lanes = slice(part % 2 * 384, (part % 2 + 1) * 384)
        refs[4][0, part // 2, :, lanes] = ordered[part * 48 : (part + 1) * 48]


def merge(scalars, slots):
    vmem = pl.BlockSpec(memory_space=pltpu.VMEM)
    return pl.pallas_call(
        merge_kernel,
        in_specs=[pl.BlockSpec(memory_space=pltpu.SMEM)] + [vmem] * 4,
        out_shape=jax.ShapeDtypeStruct((1, 2, 48, TOKENS), BF16),
        compiler_params=pltpu.CompilerParams(vmem_limit_bytes=8 * MIB),
        cost_estimate=pl.CostEstimate(flops=10**7, bytes_accessed=3 * 10**5, transcendentals=0),
    )(scalars, *slots)


def gather_plane(place, kept, sent, beside, work, crossing=False):
    block = jnp.concatenate([kept, shifted(sent, (3, 3), 1)], axis=0)
    slots = [block] + [shifted(block, (1, 1), step) for step in (1, 2, -1)]
    if crossing:
        *slots, beside = lax.optimization_barrier((*slots, beside))
        beside = cross(beside)
    block = jnp.concatenate(ring(merge(place, slots), (0, 2)), axis=0)
    block, beside = lax.optimization_barrier((block, beside))
    blocks = ring(block, (2, 0))
    done = work(beside)
    others = [shifted(block, (3, 3), 1)]
    for at in (3, 1, 2):
        blocks[at], done = lax.optimization_barrier((blocks[at], done))
    others += [shifted(blocks[at], (3, 3), 1) for at in (1, 2, 3)]
    return blocks + others, done


def split(values):
    high = values.astype(BF16)
    return high, (values - high.astype(F32)).astype(BF16)


def dot(a, b, dims=NN):
    return lax.dot_general(a, b, dims, preferred_element_type=F32)


def dot_split(a, b_both):
    both = dot(a, b_both)
    return both[:, :HD] + both[:, HD:]


def side_by_side(values):
    return jnp.concatenate(split(values), axis=1)


def stacked(weight):
    high, low = split(weight)
    return jnp.concatenate(
        [jnp.concatenate([high, low], axis=1), jnp.concatenate([high, low * 0], axis=1)], axis=0
    )


def bias_of(w_bias, normed):
    high, low = split(w_bias)
    rows = jnp.concatenate(
        [jnp.concatenate([high, high], axis=1), jnp.concatenate([low, low * 0], axis=1)], axis=0
    )
    both = dot(rows, side_by_side(normed), NT)
    return both[:HEADS] + both[HEADS:]


def standardize(values):
    mean = jnp.full((2 * HD, HD), 1.0 / HD, BF16)
    centred = values - dot(side_by_side(values), mean)
    spread = dot(side_by_side(centred * centred), mean)
    return centred * lax.rsqrt(spread + EPSILON)


def normalize(values, gain, shift):
    return standardize(values) * gain + shift


def encode(values):
    size = jnp.floor(jnp.log(1.0 + CURVE * jnp.abs(values)) * (1 / CODE_STEP) + 0.5)
    return jnp.where(values < 0, -size, size)


def decode(codes):
    size = (jnp.exp(jnp.abs(codes) * CODE_STEP) - 1.0) * (1 / CURVE)
    return jnp.where(codes < 0, -size, size)


def put_bias(bias, rows_ref, step, count):
    for row in range(count):

        @pl.when(step == row)
        def _():
            for part in range(4):
                pair, half = part // 2, part % 2
                at = pair * 24 + half * 12 + row * 2
                lanes = slice(half * 384, (half + 1) * 384)
                rows_ref[at : at + 2, :] = bias[pair * 2 : pair * 2 + 2, lanes]


def hand_over(scalar_ref, rows_ref, kept_ref, sent_ref):
    first, second = rows_ref[:24, :].astype(BF16), rows_ref[24:48, :].astype(BF16)
    kept_ref[...] = jnp.where(scalar_ref[3] == 0, first, second)
    sent_ref[...] = jnp.where(scalar_ref[3] == 0, second, first)


def bias_kernel(scalar_ref, x_ref, gain_ref, shift_ref, w_ref, kept_ref, sent_ref, rows_ref):
    step = pl.program_id(0)
    cells = x_ref[...].reshape(BIAS_ROWS * TOKENS, HD)
    bias = bias_of(w_ref[0], normalize(cells, gain_ref[0:1, :], shift_ref[0:1, :]))
    for row in range(BIAS_ROWS):
        own = bias[:, row * TOKENS : (row + 1) * TOKENS]
        put_bias(own, rows_ref, step * BIAS_ROWS + row, ROWS)

    @pl.when(step == ROWS // BIAS_ROWS - 1)
    def _():
        hand_over(scalar_ref, rows_ref, kept_ref, sent_ref)


def small(*shape):
    return pl.BlockSpec(shape, lambda i: (0,) * len(shape))


def first_bias(scalars, x, gain, shift, w_bias):
    return pl.pallas_call(
        bias_kernel,
        grid=(ROWS // BIAS_ROWS,),
        in_specs=[
            pl.BlockSpec(memory_space=pltpu.SMEM),
            pl.BlockSpec((BIAS_ROWS, TOKENS, HD), lambda i: (i, 0, 0)),
            small(2, HD),
            small(2, HD),
            small(2, HEADS, HD),
        ],
        out_specs=[small(24, 384)] * 2,
        out_shape=[jax.ShapeDtypeStruct((24, 384), BF16)] * 2,
        scratch_shapes=[pltpu.VMEM((56, 384), F32)],
        compiler_params=pltpu.CompilerParams(
            vmem_limit_bytes=60 * MIB, dimension_semantics=("arbitrary",)
        ),
        cost_estimate=pl.CostEstimate(flops=10**8, bytes_accessed=2 * 10**6, transcendentals=0),
    )(scalars, x, gain, shift, w_bias)


def lane_group():
    return lax.broadcasted_iota(jnp.int32, (1, HD), 1) // HEAD_DIM


def spreader(source_of):
    row = lax.broadcasted_iota(jnp.int32, (2 * HD, HEADS * HD), 0)
    column = lax.broadcasted_iota(jnp.int32, (2 * HD, HEADS * HD), 1)
    head, group, d = column // HD, (column // HEAD_DIM) % 4, column % HEAD_DIM
    part = source_of(head, group)
    hit = (part >= 0) & (row == part * HD + head * HEAD_DIM + d)
    return jnp.where(hit, 1.0, 0.0).astype(BF16)


def prepare_weights(weights, w_ref, spread_ref):
    for at, weight in enumerate(weights):
        w_ref[at] = stacked(weight)
    spread_ref[0] = spreader(lambda head, group: group % 2)
    spread_ref[1] = spreader(lambda head, group: group // 2)


def project_kernel(
    crossed, x_ref, gain_ref, shift_ref, gs_ref, wq_ref, wk_ref, wv_ref, wg_ref, q_ref, k_ref, v_ref, g_ref,
    w_ref, spread_ref, *rest,
):
    step = pl.program_id(0)

    @pl.when(step == 0)
    def _():
        weights = [wq_ref[0] * (HEAD_DIM**-0.5 * LOG2E), wk_ref[0], wv_ref[0], wg_ref[0]]
        prepare_weights(weights, w_ref, spread_ref)

    if crossed:
        for row in range(ROWS):
            rest[0][pl.ds(row, DEVICES, stride=ROWS), :] = x_ref[
                pl.ds(row * ROWS + step, DEVICES, stride=PADDED), :
            ]
        standard = decode(rest[0][...])
    else:
        standard = standardize(x_ref[0])
    own = slice(int(crossed), int(crossed) + 1)
    cells = side_by_side(standard * gain_ref[own, :] + shift_ref[own, :])

    def columns(at):
        return dot_split(cells, w_ref[at])

    for at, ref in enumerate((q_ref, k_ref)):
        parts = side_by_side(columns(at))
        for pair in range(2):
            cut = slice(pair * 2 * HD, (pair + 1) * 2 * HD)
            spread = dot(parts, spread_ref[at, :, cut]).astype(BF16)
            ref[0, 2 * pair] = spread[:, :HD]
            ref[0, 2 * pair + 1] = spread[:, HD:]
    v_ref[0] = side_by_side(columns(2))
    g_ref[0] = jax.nn.sigmoid(columns(3) + gs_ref[own, :])


def matrix(second):
    return pl.BlockSpec((1, HD, HD), lambda i: (int(second), 0, 0))


def project(crossed, x, vectors, matrices):
    whole = pl.BlockSpec(memory_space=pltpu.VMEM)
    row_spec = pl.BlockSpec((1, TOKENS, HD), lambda i: (i, 0, 0))
    head_spec = pl.BlockSpec((1, HEADS, TOKENS, HD), lambda i: (i, 0, 0, 0))
    scratch = [
        pltpu.VMEM((4, 2 * HD, 2 * HD), BF16),
        pltpu.VMEM((2, 2 * HD, HEADS * HD), BF16),
    ]
    if crossed:
        scratch.append(pltpu.VMEM((TOKENS, HD), F32))
    return pl.pallas_call(
        functools.partial(project_kernel, crossed),
        grid=(ROWS,),
        in_specs=[whole if crossed else row_spec] + [small(2, HD)] * 3 + [matrix(crossed)] * 4,
        out_specs=[
            head_spec, head_spec, pl.BlockSpec((1, TOKENS, 2 * HD), lambda i: (i, 0, 0)), row_spec,
        ],
        out_shape=[
            jax.ShapeDtypeStruct((ROWS, HEADS, TOKENS, HD), BF16),
            jax.ShapeDtypeStruct((ROWS, HEADS, TOKENS, HD), BF16),
            jax.ShapeDtypeStruct((ROWS, TOKENS, 2 * HD), BF16),
            jax.ShapeDtypeStruct((ROWS, TOKENS, HD), F32),
        ],
        scratch_shapes=scratch,
        compiler_params=pltpu.CompilerParams(
            vmem_limit_bytes=24 * MIB, dimension_semantics=("arbitrary",)
        ),
        cost_estimate=pl.CostEstimate(
            flops=10**10, bytes_accessed=17 * 10**6, transcendentals=10**6
        ),
    )(x, *vectors, *matrices)


def build_plane(scalar_ref, piece_refs, plane_ref, flat_ref, turned):
    my_x, my_z, core, real = scalar_ref[0], scalar_ref[2], scalar_ref[3], scalar_ref[4]
    limit = ((real + 255) // 256) * 256

    def one_slot(inner, _):
        for ref, outer, pair in zip(piece_refs, (0, 1, 2, 3) * 2, (core,) * 4 + (1 - core,) * 4):
            x = (my_x - jnp.where(pair == 0, inner, outer)) & 3
            z = (my_z - jnp.where(pair == 0, outer, inner)) & 3
            group = (x & 1) * 8 + z * 2 + x // 2
            rows = pl.ds(pl.multiple_of(group * 48, 16), 48)
            for half in range(2):
                lanes = slice(half * 384, (half + 1) * 384)

                @pl.when(group * 48 < limit if turned else half * 384 < limit)
                def _():
                    for odd in range(2):
                        values = ref[inner, odd, :, lanes]
                        if turned:
                            flat_ref[pair * 2 + odd, rows, lanes] = values
                        else:
                            key = lax.broadcasted_iota(jnp.int32, (48, 384), 1) + half * 384
                            plane_ref[pair * 2 + odd, rows, lanes] = jnp.where(
                                key < real, values.astype(F32) * LOG2E, NEGATIVE
                            )
        return 0

    lax.fori_loop(0, 4, one_slot, 0)

    def turn(head, _):
        for block in range(6):
            keys = slice(block * 128, block * 128 + 128)

            @pl.when(block * 128 < limit)
            def _():
                live = lax.broadcasted_iota(jnp.int32, (128, 128), 1) + block * 128 < real
                for other in range(6):
                    rows = slice(other * 128, other * 128 + 128)
                    values = flat_ref[head, keys, rows].T.astype(F32) * LOG2E
                    plane_ref[head, rows, keys] = jnp.where(live, values, NEGATIVE)
        return 0

    if turned:
        lax.fori_loop(0, HEADS, turn, 0)


def attend(keys, q_ref, k_ref, v_ref, plane_ref):
    group = lane_group()
    value = total = None
    for head in range(HEADS):
        scores = dot(q_ref[0, head], k_ref[0, head, :keys, :], NT) + plane_ref[head, :, :keys]
        highest = jnp.max(scores, axis=-1, keepdims=True)
        weights = jnp.exp2(scores - highest).astype(BF16)
        weight = jnp.sum(weights.astype(F32), axis=-1, keepdims=True)
        mixed = dot(weights, v_ref[0, :keys, :])
        mixed = mixed[:, :HD] + mixed[:, HD:]
        weight = jnp.broadcast_to(weight, mixed.shape)
        value = mixed if head == 0 else jnp.where(group == head, mixed, value)
        total = weight if head == 0 else jnp.where(group == head, weight, total)
    return value / total


def attend_kernel(turned, scalar_ref, q_ref, k_ref, v_ref, g_ref, wo_ref, *rest):
    piece_refs, rest = rest[:8], rest[8:]
    step = pl.program_id(0)
    before = jnp.maximum(step - 1, 0)
    if turned:
        crossed_ref, plane_ref, mixed_ref, gated_ref, flat_ref = rest
    else:
        x_ref, gain_ref, shift_ref, nbias_ref = rest[:4]
        first_ref, crossed_ref, kept_ref, sent_ref = rest[4:8]
        plane_ref, mixed_ref, gated_ref, rows_ref, wide_ref, bias_ref = rest[8:]

    @pl.when(step == 0)
    def _():
        gated_ref[...] = jnp.zeros_like(gated_ref)
        build_plane(scalar_ref, piece_refs, plane_ref, flat_ref if turned else None, turned)
        if not turned:
            wide_ref[...] = jnp.zeros_like(wide_ref)

    def finish():
        update = dot_split(gated_ref[...], stacked(wo_ref[0]))
        if turned:
            mixed_ref[...] = update
            for row in range(ROWS):
                crossed_ref[pl.ds(row * ROWS + before, DEVICES, stride=PADDED), :] = mixed_ref[
                    pl.ds(row, DEVICES, stride=ROWS), :
                ]
        else:
            first = x_ref[0] + update
            first_ref[0] = first
            standard = standardize(first)
            mixed_ref[...] = encode(standard)
            for column in range(ROWS):
                wide_ref[pl.ds(before * ROWS + column, DEVICES, stride=PADDED), :] = mixed_ref[
                    pl.ds(column, DEVICES, stride=ROWS), :
                ]
            normed = standard * gain_ref[1:2, :] + shift_ref[1:2, :]
            bias_ref[:HEADS, :] = bias_of(nbias_ref[1], normed)

    real = scalar_ref[4]
    for keys in (256, 512, 768):

        @pl.when((step < ROWS) & (real > keys - 256) & (real <= keys))
        def _():
            finish()
            mixed = attend(keys, q_ref, k_ref, v_ref, plane_ref)
            gated_ref[...] = side_by_side(g_ref[0] * mixed)

    @pl.when(step == ROWS)
    def _():
        finish()

    if not turned:
        put_bias(bias_ref[:HEADS, :], rows_ref, step - 1, ROWS)

        @pl.when(step == ROWS)
        def _():
            crossed_ref[...] = wide_ref[...].astype(jnp.int32).astype(jnp.int16)
            hand_over(scalar_ref, rows_ref, kept_ref, sent_ref)


def run_pass(turned, scalars, projected, w_o, pieces, x=None, extra=()):
    whole = pl.BlockSpec(memory_space=pltpu.VMEM)
    now, last = (lambda i: jnp.minimum(i, ROWS - 1)), (lambda i: jnp.maximum(i - 1, 0))
    row_spec = pl.BlockSpec((1, TOKENS, HD), lambda i: (now(i), 0, 0))
    last_spec = pl.BlockSpec((1, TOKENS, HD), lambda i: (last(i), 0, 0))
    head_spec = pl.BlockSpec((1, HEADS, TOKENS, HD), lambda i: (now(i), 0, 0, 0))
    in_specs = [pl.BlockSpec(memory_space=pltpu.SMEM), head_spec, head_spec]
    in_specs += [pl.BlockSpec((1, TOKENS, 2 * HD), lambda i: (now(i), 0, 0)), row_spec]
    in_specs += [matrix(turned)] + [whole] * 8
    out_shape = [jax.ShapeDtypeStruct((DEVICES * PADDED, HD), F32 if turned else jnp.int16)]
    out_specs = [pl.BlockSpec((DEVICES * PADDED, HD), lambda i: (0, 0))]
    scratch = [pltpu.VMEM((HEADS, TOKENS, TOKENS), F32), pltpu.VMEM((TOKENS, HD), F32)]
    scratch.append(pltpu.VMEM((TOKENS, 2 * HD), BF16))
    if turned:
        scratch.append(pltpu.VMEM((HEADS, TOKENS, TOKENS), BF16))
    args = [scalars, *projected, w_o, *pieces]
    if not turned:
        in_specs += [last_spec, small(2, HD), small(2, HD), small(2, HEADS, HD)]
        args += [x, *extra]
        out_shape = [jax.ShapeDtypeStruct((ROWS, TOKENS, HD), F32)] + out_shape
        out_shape += [jax.ShapeDtypeStruct((24, 384), BF16)] * 2
        out_specs = [last_spec] + out_specs + [pl.BlockSpec((24, 384), lambda i: (0, 0))] * 2
        scratch += [pltpu.VMEM((56, 384), F32), pltpu.VMEM((DEVICES * PADDED, HD), F32)]
        scratch.append(pltpu.VMEM((8, TOKENS), F32))
    return pl.pallas_call(
        functools.partial(attend_kernel, turned),
        grid=(ROWS + 1,),
        in_specs=in_specs,
        out_specs=out_specs,
        out_shape=out_shape,
        scratch_shapes=scratch,
        compiler_params=pltpu.CompilerParams(
            vmem_limit_bytes=26 * MIB, dimension_semantics=("arbitrary",)
        ),
        cost_estimate=pl.CostEstimate(
            flops=2 * 10**10, bytes_accessed=2 * 10**7, transcendentals=14 * 10**6
        ),
    )(*args)


def final_kernel(first_ref, update_ref, out_ref, row_ref):
    step = pl.program_id(0)
    for column in range(ROWS):
        row_ref[pl.ds(column, DEVICES, stride=ROWS), :] = update_ref[
            pl.ds(step * ROWS + column, DEVICES, stride=PADDED), :
        ]
    out_ref[0] = first_ref[0] + row_ref[...]


def add_crossed(first, update):
    row_spec = pl.BlockSpec((1, TOKENS, HD), lambda i: (i, 0, 0))
    return pl.pallas_call(
        final_kernel,
        grid=(ROWS,),
        in_specs=[row_spec, pl.BlockSpec(memory_space=pltpu.VMEM)],
        out_specs=row_spec,
        out_shape=jax.ShapeDtypeStruct((ROWS, TOKENS, HD), F32),
        scratch_shapes=[pltpu.VMEM((TOKENS, HD), F32)],
        compiler_params=pltpu.CompilerParams(
            vmem_limit_bytes=16 * MIB, dimension_semantics=("arbitrary",)
        ),
        cost_estimate=pl.CostEstimate(flops=10**6, bytes_accessed=8 * 10**6, transcendentals=0),
    )(first, update)


def cross(values):
    return lax.all_to_all(values, AXES, split_axis=0, concat_axis=0, tiled=True)


def on_device(
    pair_tensor,
    token_mask,
    ln_gain,
    ln_shift,
    w_query,
    w_key,
    w_value,
    w_bias,
    w_gate,
    gate_shift,
    w_out,
):
    row, col = lax.axis_index("row"), lax.axis_index("col")
    place = [(col // 8) * 2 + row // 4, (col // 2) % 4, row % 4, col % 2]
    place = jnp.stack([jnp.int32(p) for p in place])
    vectors, matrices = (ln_gain, ln_shift, gate_shift), (w_query, w_key, w_value, w_gate)

    start = first_bias(place, pair_tensor, ln_gain, ln_shift, w_bias)
    scalars = jnp.concatenate([place, jnp.sum(token_mask, dtype=jnp.int32, keepdims=True)])
    planes, (projected, scalars) = gather_plane(
        place, *start, (pair_tensor, scalars),
        lambda held: (project(False, held[0], vectors, matrices), held[1]),
    )
    first, codes, *end = run_pass(
        False, scalars, projected, w_out, planes, pair_tensor, (ln_gain, ln_shift, w_bias)
    )
    planes, projected = gather_plane(
        place, *end, codes, lambda held: project(True, held.astype(F32), vectors, matrices), True
    )
    (update,) = run_pass(True, scalars, projected, w_out, planes)
    return add_crossed(first, cross(update.astype(jnp.float16)).astype(F32))


def solution(mesh):
    placed = (P(AXES, None, None), P(), P(), P(), P(), P(), P(), P(), P(), P(), P())
    return jax.shard_map(
        on_device,
        mesh=mesh,
        in_specs=placed,
        out_specs=P(AXES, None, None),
        check_vma=False,
    )
```
